512 devices in a mesh: gx: 16 (over z), gy: 32 (over y, x, core).
Axes of the slice: x: 4, y: 4, z: 16, core: 2. Of those that a mesh axis runs over, the one named last changes fastest.
Arguments:
- source: float32 [128, 256, 256], P('gx', 'gy'), may hold values from -5 to 5
- kappa: float32 [128, 256, 256], P('gx', 'gy'), may hold values from 0.3 to 3
Outputs:
- fine_solution: float32 [128, 256, 256], P('gx', 'gy')
- coarse_solution: float32 [64, 128, 128], P('gx', 'gy')
The draws below stay inside these ranges and needn't reach their ends.
All inputs are finite; a program needn't handle non-finite values.
Results may differ from the reference program's by a relative error of at most 0.00015.
Values sent between devices are 32-bit elements; how exact they have to be, the bound alone decides.
A program may use at most 64 MiB of HBM per device.

```python
import math
import jax
import jax.numpy as jnp
from jax import lax

NZ = 256
LEVELS = 3
PRE = 2
POST = 2
CSWEEPS = 8
NX = 128
NY = 256


def draw_source(key, part):
    key = jax.random.fold_in(key, 7)
    shape = (NX, NY, NZ)
    pos_x = (jnp.arange(NX, dtype=jnp.float32) + 0.5) / NX
    pos_y = (jnp.arange(NY, dtype=jnp.float32) + 0.5) / NY
    pos_z = (jnp.arange(NZ, dtype=jnp.float32) + 0.5) / NZ
    smooth_part = jnp.sin(jnp.pi * pos_x)[:, None, None] * jnp.sin(jnp.pi * pos_y)[None, :, None] * jnp.sin(jnp.pi * pos_z)[None, None, :]
    rough = jax.random.truncated_normal(key, -4.0, 4.0, shape, jnp.float32)
    return rough + 0.02 * smooth_part


def shard_levels(own_key, extent, split, least, high):
    def one(axis_at, blocks):
        heights = jax.random.uniform(jax.random.fold_in(jax.random.fold_in(own_key, 6), axis_at), (blocks,), jnp.float32, least / len(split), high / len(split))
        return jnp.repeat(jnp.exp(heights), extent[axis_at] // blocks).reshape((-1,) + (1,) * (len(extent) - axis_at - 1))

    level = one(*split[0])
    for cut in split[1:]:
        level = level * one(*cut)
    return level


def setup_inputs(seed: int = 0) -> dict:
    arg_keys = jax.random.split(jax.random.key(seed), 3)
    source = draw_source(jax.random.fold_in(arg_keys[2], 71), 0)
    kappa = jnp.clip(jnp.exp(math.log(3.0) - 2.3025851 * jax.random.uniform(arg_keys[1], (NX, NY, NZ), jnp.float32) ** shard_levels(arg_keys[1], (NX, NY, NZ), ((0, 16), (1, 32)), -0.2, 0.2)), 0.3, 3.0)
    return {"source": source, "kappa": kappa}


OMEGA = 0.8

def restrict(field):
    lead = field.shape[:-3]
    size_a, size_b, size_c = field.shape[-3:]
    blocks = field.reshape(lead + (size_a // 2, 2, size_b // 2, 2, size_c // 2, 2))
    return blocks.mean(axis=(-5, -3, -1))

def prolong(field):
    return jnp.repeat(jnp.repeat(jnp.repeat(field, 2, -3), 2, -2), 2, -1)

def stencil_faces(padded):
    centre = padded[..., 1:-1, 1:-1, 1:-1]
    face_west = 0.5 * (centre + padded[..., :-2, 1:-1, 1:-1])
    face_east = 0.5 * (centre + padded[..., 2:, 1:-1, 1:-1])
    face_south = 0.5 * (centre + padded[..., 1:-1, :-2, 1:-1])
    face_north = 0.5 * (centre + padded[..., 1:-1, 2:, 1:-1])
    face_below = 0.5 * (centre + padded[..., 1:-1, 1:-1, :-2])
    face_above = 0.5 * (centre + padded[..., 1:-1, 1:-1, 2:])
    total = face_west + face_east + face_south + face_north + face_below + face_above
    return (face_west, face_east, face_south, face_north, face_below, face_above, total)

def neighbours(padded, field, coeff):
    beside = coeff[0] * padded[..., :-2, 1:-1, 1:-1] + coeff[1] * padded[..., 2:, 1:-1, 1:-1]
    beside = beside + coeff[2] * padded[..., 1:-1, :-2, 1:-1] + coeff[3] * padded[..., 1:-1, 2:, 1:-1]
    beside = beside + coeff[4] * padded[..., 1:-1, 1:-1, :-2] + coeff[5] * padded[..., 1:-1, 1:-1, 2:]
    return coeff[6] * field - beside

def operate(field, level_data):
    coeff = stencil_faces(level_data[0])
    return neighbours(jnp.pad(field, 1), field, coeff)

def sweeps(field, rhs_field, level_data, count):
    for repeat in range(count):
        field = field + OMEGA * (rhs_field - operate(field, level_data)) / level_data[1]
    return field

def inner(left, right):
    return lax.optimization_barrier(jnp.sum(left * right, axis=(-3, -2, -1), keepdims=True))

def conjgrad(rhs_field, operator):
    field = jnp.zeros_like(rhs_field)
    resid = rhs_field
    direction = rhs_field
    norm_now = inner(resid, resid)
    for repeat in range(CSWEEPS):
        image = operator(direction)
        alpha = norm_now / inner(direction, image)
        field = field + alpha * direction
        resid = resid - alpha * image
        norm_next = inner(resid, resid)
        direction = resid + norm_next / norm_now * direction
        norm_now = norm_next
    return field

def vcycle(section, rhs_field, levels_data):
    level_data = levels_data[section]
    if section == LEVELS:
        return conjgrad(rhs_field, lambda item: operate(item, level_data))
    field = OMEGA * rhs_field / level_data[1]
    field = sweeps(field, rhs_field, level_data, PRE - 1)
    resid = rhs_field - operate(field, level_data)
    correction = vcycle(section + 1, 4.0 * restrict(resid), levels_data)
    field = field + prolong(correction)
    return sweeps(field, rhs_field, level_data, POST)

def reference(source, kappa):
    kappas = [kappa]
    for section in range(LEVELS):
        kappas.append(restrict(kappas[-1]))
    levels_data = []
    for item in kappas:
        padded = jnp.pad(item, 1)
        levels_data.append((padded, stencil_faces(padded)[6]))
    fine_solution = vcycle(0, source, levels_data)
    coarse_solution = vcycle(1, 4.0 * restrict(source), levels_data)
    return (fine_solution, coarse_solution)
```

```python
import jax
import jax.numpy as jnp
from jax import lax
from jax.experimental import pallas as pl
from jax.experimental.pallas import tpu as pltpu
from jax.sharding import PartitionSpec as P


CSWEEPS = 8
OMEGA = 0.8
F32 = jnp.float32
ROWS = 16

INNER = [(dx, dy) for dx in (-1, 1, 0) for dy in (0, -1, 1) if (dx, dy) != (0, 0)]
AROUND = INNER + [
    (dx, dy) for dx in (-2, 2, -1, 1, 0) for dy in (-2, -1, 0, 1, 2) if max(abs(dx), abs(dy)) == 2
]

(G_K0, G_S0, G_E1, G_K2, G_ZK, G_GK, G_B1, G_B2, G_ZB, G_GB, G_V0, G_V1, G_U2) = range(13)
GROUPS = 13


def span(step, size, rim):
    low = max(0, step * size - rim)
    high = min(size, size + rim + step * size)
    return low, high - low, low - step * size


def roll(x, shift, axis):
    return pltpu.roll(x, shift % x.shape[axis], axis)


def iota(shape, axis):
    return lax.broadcasted_iota(jnp.int32, shape, axis)


def take_lanes(x, index):
    return jnp.take_along_axis(x, index, axis=1)


def take_rows(x, index):
    return jnp.take_along_axis(x, index, axis=0)


def pair_lanes(a, b):
    lane = iota(a.shape, 1)
    index = lax.rem(2 * lane, 128)
    a = take_lanes(a + roll(a, -1, 1), index)
    if b is None:
        return a
    b = take_lanes(b + roll(b, -1, 1), index)
    return jnp.where(lane < 64, a, b)


def pair_rows(x):
    return take_rows(x + roll(x, -1, 0), lax.rem(2 * iota(x.shape, 0), 8))


def kernel(nx, ny, src_hbm, kap_hbm, fine_ref, coarse_ref, K0, S0, V0, VA0, VB0, C0, E1, B1, V1, VA1, VB1, C1, M1,
           K2, B2, U2, VA2, VB2, C2, M2, ZK, ZB, GK, GB, C3, R3, W3, P3, Q3, X3, S5, T5, D, local_sem, send_sem, recv_sem):
    gx = lax.axis_index("gx")
    gy = lax.axis_index("gy")
    mesh_ids = pl.DeviceIdType.MESH

    def peer(dx, dy):
        return (lax.rem(gx + (dx + nx), nx) if not isinstance(dx, int) or dx else gx,
                lax.rem(gy + (dy + ny), ny) if not isinstance(dy, int) or dy else gy)

    sent = [0]

    def wait_rows(rows, sem):
        pltpu.make_async_copy(D.at[pl.ds(0, rows)], D.at[pl.ds(0, rows)], sem).wait()

    def wait_group(group, rows):
        wait_rows(rows, recv_sem.at[group])

    def ship(group, ref, lead, steps, size, rim, corner, offset):
        total = 0
        for dx, dy in steps:
            reach = corner if dx and dy else rim
            px, cx, qx = span(dx, size, reach)
            py, cy, qy = span(dy, size, reach)
            here = (pl.ds(px + offset, cx), pl.ds(py, cy), slice(None))
            there = (pl.ds(qx + offset, cx), pl.ds(qy % ROWS, cy), slice(None))
            if lead is not None:
                here, there = (pl.ds(*lead),) + here, (pl.ds(*lead),) + there
            pltpu.make_async_remote_copy(
                src_ref=ref.at[here], dst_ref=ref.at[there], send_sem=send_sem.at[group], recv_sem=recv_sem.at[group],
                device_id=peer(dx, dy), device_id_type=mesh_ids,
            ).start()
            total += cx * cy * (ref.shape[-1] // 128) * (lead[1] if lead else 1)
        return total

    def ship_column(group, ref):
        def step(i, carry):
            pltpu.make_async_remote_copy(
                src_ref=ref.at[pl.ds(gx, 1)], dst_ref=ref.at[pl.ds(gx, 1)], send_sem=send_sem.at[group],
                recv_sem=recv_sem.at[group], device_id=(lax.rem(gx + i, nx), gy), device_id_type=mesh_ids,
            ).start()
            return carry
        lax.fori_loop(1, nx, step, 0)
        return nx - 1

    def ship_row(group, ref):
        def step(i, carry):
            pltpu.make_async_remote_copy(
                src_ref=ref.at[gy], dst_ref=ref.at[gy], send_sem=send_sem.at[group],
                recv_sem=recv_sem.at[group], device_id=(gx, lax.rem(gy + i, ny)), device_id_type=mesh_ids,
            ).start()
            return carry
        lax.fori_loop(1, ny, step, 0)
        return 8 * (ny - 1)

    copies = [
        pltpu.make_async_copy(kap_hbm, K0.at[pl.ds(3, 8), pl.ds(0, 8), :], local_sem.at[0]),
        pltpu.make_async_copy(src_hbm, S0.at[pl.ds(2, 8), pl.ds(0, 8), :], local_sem.at[1]),
    ]
    for copy in copies:
        copy.start()
    barrier = pltpu.get_barrier_semaphore()

    def greet(device):
        pl.semaphore_signal(barrier, inc=1, device_id=device, device_id_type=mesh_ids)

    def greet_x(i, carry):
        greet((lax.rem(gx + i, nx), gy))
        return carry

    def greet_y(i, carry):
        greet((gx, lax.rem(gy + i, ny)))
        return carry

    lax.fori_loop(1, nx, greet_x, 0)
    lax.fori_loop(1, ny, greet_y, 0)
    diagonal = [(dx, dy) for dx, dy in AROUND if dx and dy]
    for dx, dy in diagonal:
        greet(peer(dx, dy))
    for copy in copies:
        copy.wait()
    pl.semaphore_wait(barrier, nx - 1 + ny - 1 + len(diagonal))

    n_k0 = ship(G_K0, K0, None, INNER, 8, 3, 2, 3)
    n_s0 = ship(G_S0, S0, None, INNER, 8, 2, 1, 2)

    def restrict0(ref, offset, scale):
        out = []
        for i in range(4):
            both = ref[offset + 2 * i, 0:8, :] + ref[offset + 2 * i + 1, 0:8, :]
            out.append(scale * pair_rows(pair_lanes(both[:, :128], both[:, 128:])))
        return out

    own1 = restrict0(K0, 3, 0.125)
    for i, tile in enumerate(own1):
        E1[1, 3 + i, 0:4, :] = tile[0:4]
    for i, tile in enumerate(restrict0(S0, 2, 0.5)):
        E1[0, 3 + i, 0:4, :] = tile[0:4]
    n_e1 = ship(G_E1, E1, (0, 2), INNER, 4, 3, 3, 3)
    own2 = []
    for i in range(2):
        own2.append(0.125 * pair_rows(pair_lanes(own1[2 * i] + own1[2 * i + 1], None)))
        K2[4 + i, 0:2, :] = own2[i][0:2]
    n_k2 = ship(G_K2, K2, None, AROUND, 2, 4, 4, 4)
    both = own2[0] + own2[1]
    ZK[pl.ds(gx, 1), :] = 0.125 * pair_rows(pair_lanes(both, None))[0:1]
    n_zk = ship_column(G_ZK, ZK)

    def inside(shape, first, size, rim):
        plane = iota(shape, 0) + first + gx * size
        row = iota(shape, 1)
        row = jnp.where(row < 8 + size // 2, row, row - ROWS)
        good = (row >= -rim) & (row < size + rim)
        row = row + gy * size
        return good & (plane >= 0) & (plane < nx * size) & (row >= 0) & (row < ny * size)

    def faces(read, C, planes, width, depth, size, rim, first, chunk):
        for a in range(0, planes, chunk):
            n = min(chunk, planes - a)
            k = read(a, n + 2)
            mid = k[1:n + 1]
            west = 0.5 * (k[0:n + 1] + k[1:n + 2])
            C[0, a:a + n + 1] = west
            north = 0.5 * (mid + roll(mid, -1, 1))
            south = roll(north, 1, 1)
            z = lax.rem(iota(mid.shape, 2), depth)
            top = z == depth - 1
            bottom = z == 0
            above = 0.5 * (mid + jnp.where(top, 0.0, roll(mid, -1, 2)))
            below = 0.5 * (mid + jnp.where(bottom, 0.0, roll(mid, 1, 2)))
            total = west[0:n] + west[1:n + 1] + north + south + above + below
            C[1, a:a + n] = north
            C[2, a:a + n] = south
            C[3, a:a + n] = jnp.where(top, 0.0, above)
            C[4, a:a + n] = jnp.where(bottom, 0.0, below)
            C[5, a:a + n] = total
            C[6, a:a + n] = jnp.where(inside(mid.shape, first + a, size, rim), OMEGA / total, 0.0)

    def residual(v, b, C, c, n, rows=ROWS):
        mid = v[1:n + 1]
        cut = slice(0, rows)
        beside = C[0, c:c + n, cut] * v[0:n, cut] + C[0, c + 1:c + n + 1, cut] * v[2:n + 2, cut]
        beside += C[1, c:c + n, cut] * roll(mid, -1, 1)[:, cut] + C[2, c:c + n, cut] * roll(mid, 1, 1)[:, cut]
        mid = mid[:, cut]
        beside += C[3, c:c + n, cut] * roll(mid, -1, 2) + C[4, c:c + n, cut] * roll(mid, 1, 2)
        return b - C[5, c:c + n, cut] * mid + beside

    def sweep(V, vo, b, C, co, store, first, planes, chunk, rows=ROWS):
        for a in range(0, planes, chunk):
            n = min(chunk, planes - a)
            p = first + a
            v = V(p - 1, n + 2)
            r = residual(v, b(p, n, rows), C, p + co, n, rows)
            store(p, n, v[1:n + 1, 0:rows] + C[6, p + co:p + co + n, 0:rows] * r)

    wait_group(G_K0, n_k0)

    def read_k0(a, n):
        k = K0[a:a + n]
        return jnp.where(inside(k.shape, a - 3, 8, 3), k, 0.0)

    faces(read_k0, C0, 12, 256, 256, 8, 3, -2, 2)
    wait_group(G_S0, n_s0)
    for a in range(0, 12, 2):
        VA0[a:a + 2] = C0[6, a:a + 2] * S0[a:a + 2]

    def at(ref, offset, lead=None):
        def read(p, n, rows=ROWS):
            where = (pl.ds(p + offset, n), pl.ds(0, rows), slice(None))
            return ref[where] if lead is None else ref[(lead,) + where]
        return read

    def to(ref, offset, lead=None):
        def store(p, n, x):
            where = (pl.ds(p + offset, n), pl.ds(0, x.shape[1]), slice(None))
            if lead is None:
                ref[where] = x
            else:
                ref[(lead,) + where] = x
        return store

    sweep(at(VA0, 2), 2, at(S0, 2), C0, 2, to(VB0, 1), -1, 10, 2)
    for i in range(4):
        r = residual(VB0[2 * i:2 * i + 4], S0[2 + 2 * i:4 + 2 * i, 0:8], C0, 2 + 2 * i, 2, 8)
        both = r[0] + r[1]
        B1[3 + i, 0:4, :] = 0.5 * pair_rows(pair_lanes(both[:, :128], both[:, 128:]))[0:4]
    n_b1 = ship(G_B1, B1, None, INNER, 4, 2, 2, 3)
    V0[2:10, 0:8, :] = VB0[1:9, 0:8, :]

    wait_group(G_ZK, n_zk)

    def packed(ref):
        keep = lax.rem(iota((8, 128), 0) + 8 * (iota((8, 128), 1) // 64), 16) < nx
        return jnp.where(keep, jnp.where(iota((8, 128), 1) < 64, ref[0:8], ref[8:16]), 0.0)

    GK[gy] = packed(ZK)
    n_gk = ship_row(G_GK, GK)
    wait_group(G_E1, n_e1)

    def read_k1(a, n):
        k = E1[1, a:a + n]
        return jnp.where(inside(k.shape, a - 3, 4, 3), k, 0.0)

    faces(read_k1, C1, 8, 128, 128, 4, 3, -2, 4)
    b1 = (at(B1, 3), at(E1, 3, 0))

    def down1(k):
        for a in range(0, 8, 4):
            VA1[k, a:a + 4] = C1[6, a:a + 4] * b1[k](a - 2, 4)
        sweep(at(VA1, 2, k), 2, b1[k], C1, 2, to(VB1, 1, k), -1, 6, 6)
        r = residual(VB1[k], b1[k](0, 4, 8), C1, 2, 4, 8)
        V1[k, 3:7, 0:4, :] = VB1[k, 1:5, 0:4, :]
        return r[0] + r[1], r[2] + r[3]

    pairs_c = down1(1)
    wait_group(G_B1, n_b1)
    pairs_f = down1(0)
    for i in range(2):
        tile = 0.5 * pair_rows(pair_lanes(pairs_f[i], pairs_c[i]))
        B2[2 + i, 0:2, :] = tile[0:2]
        U2[0, 4 + i, 0:2, :] = tile[0:2]
    n_b2 = ship(G_B2, B2, None, INNER, 2, 2, 2, 2)

    wait_group(G_K2, n_k2)

    def read_k2(a, n):
        k = K2[a:a + n]
        return jnp.where(inside(k.shape, a - 4, 2, 4), k, 0.0)

    faces(read_k2, C2, 8, 128, 64, 2, 4, -3, 4)
    wait_group(G_B2, n_b2)
    VA2[0:6] = C2[6, 1:7] * B2[0:6]
    sweep(at(VA2, 2), 2, at(B2, 2), C2, 3, to(VB2, 1), -1, 4, 4)
    r = residual(VB2[0:4], B2[2:4, 0:8], C2, 3, 2, 8)
    U2[1, 4:6, 0:2, :] = VB2[1:3, 0:2, :]
    ZB[pl.ds(gx, 1), :] = 0.5 * pair_rows(pair_lanes(r[0] + r[1], None))[0:1]
    n_zb = ship_column(G_ZB, ZB)

    shape = (8, 128)
    sub, lane = iota(shape, 0), iota(shape, 1)
    half = lane // 64
    at_x = sub + 8 * half
    z = lax.rem(lane, 32)
    first_rhs = lax.rem(lane, 64) < 32

    def next_x(v):
        a = roll(v, -1, 1)
        return jnp.where(sub == 7, roll(a, 64, 2), a)

    def previous_x(v):
        a = roll(v, 1, 1)
        return jnp.where(sub == 0, roll(a, 64, 2), a)

    wait_group(G_GK, n_gk)
    chunk3 = min(8, ny)
    blank = jnp.zeros(shape, F32)
    for a in range(0, ny, chunk3):
        k = GK[a:a + chunk3]
        up_y = [GK[j] if j < ny else blank for j in range(a + 1, a + chunk3 + 1)]
        down_y = [GK[j] if j >= 0 else blank for j in range(a - 1, a + chunk3 - 1)]
        y_next = 0.5 * (k + jnp.stack(up_y))
        y_previous = 0.5 * (k + jnp.stack(down_y))
        x_next = 0.5 * (k + jnp.where(at_x < nx - 1, next_x(k), 0.0))
        x_previous = 0.5 * (k + jnp.where(at_x > 0, previous_x(k), 0.0))
        z_next = 0.5 * (k + jnp.where(z < 31, roll(k, -1, 2), 0.0))
        z_previous = 0.5 * (k + jnp.where(z > 0, roll(k, 1, 2), 0.0))
        C3[0, a:a + chunk3] = y_previous
        C3[1, a:a + chunk3] = y_next
        C3[2, a:a + chunk3] = jnp.where(at_x < nx - 1, x_next, 0.0)
        C3[3, a:a + chunk3] = jnp.where((at_x > 0) & (at_x < nx), x_previous, 0.0)
        C3[4, a:a + chunk3] = jnp.where(z < 31, z_next, 0.0)
        C3[5, a:a + chunk3] = jnp.where(z > 0, z_previous, 0.0)
        C3[6, a:a + chunk3] = y_next + y_previous + x_next + x_previous + z_next + z_previous
    R3[0] = blank
    R3[ny + 1] = blank

    wait_group(G_ZB, n_zb)
    GB[gy] = packed(ZB)
    n_gb = ship_row(G_GB, GB)
    n_v0 = ship(G_V0, V0, None, INNER, 8, 2, 1, 2)
    n_v1 = ship(G_V1, V1, (0, 2), INNER, 4, 3, 3, 3)
    n_u2 = ship(G_U2, U2, (0, 2), AROUND, 2, 4, 4, 4)
    for a in range(0, ny, chunk3):
        P3[a:a + chunk3] = jnp.zeros((chunk3,) + shape, F32)
        Q3[a:a + chunk3] = jnp.zeros((chunk3,) + shape, F32)
        X3[2 + a:2 + a + chunk3] = jnp.zeros((chunk3,) + shape, F32)
    wait_group(G_GB, n_gb)
    for a in range(0, ny, chunk3):
        R3[1 + a:1 + a + chunk3] = GB[a:a + chunk3]

    def over_grid(x):
        x = jnp.sum(x, axis=0, keepdims=True)
        first = jnp.sum(jnp.where(first_rhs[0:1], x, 0.0), axis=1, keepdims=True)
        second = jnp.sum(jnp.where(first_rhs[0:1], 0.0, x), axis=1, keepdims=True)
        return jnp.where(first_rhs[0:1], first, second)

    def iteration(_, carry):
        norm_before, alpha_before = carry
        norm, energy = blank, blank
        for a in range(0, ny, chunk3):
            mid = R3[1 + a:1 + a + chunk3]
            beside = C3[0, a:a + chunk3] * R3[a:a + chunk3] + C3[1, a:a + chunk3] * R3[2 + a:2 + a + chunk3]
            beside += C3[2, a:a + chunk3] * next_x(mid) + C3[3, a:a + chunk3] * previous_x(mid)
            beside += C3[4, a:a + chunk3] * roll(mid, -1, 2) + C3[5, a:a + chunk3] * roll(mid, 1, 2)
            image = C3[6, a:a + chunk3] * mid - beside
            W3[a:a + chunk3] = image
            norm += jnp.sum(mid * mid, axis=0)
            energy += jnp.sum(mid * image, axis=0)
        norm, energy = over_grid(norm), over_grid(energy)
        beta = norm / norm_before
        alpha = norm / (energy - beta * norm / alpha_before)
        for a in range(0, ny, chunk3):
            p = R3[1 + a:1 + a + chunk3] + beta * P3[a:a + chunk3]
            q = W3[a:a + chunk3] + beta * Q3[a:a + chunk3]
            P3[a:a + chunk3] = p
            Q3[a:a + chunk3] = q
            X3[2 + a:2 + a + chunk3] += alpha * p
            R3[1 + a:1 + a + chunk3] -= alpha * q
        return norm, alpha

    lax.fori_loop(0, CSWEEPS, iteration, (jnp.full((1, 128), jnp.inf, F32), jnp.ones((1, 128), F32)))

    near = X3[pl.ds(gy, 5)]
    S5[:, 2:10, :] = near
    S5[:, 10:18, :] = roll(near, 64, 2)
    for dx in range(-2, 3):
        for dy in range(-2, 3):
            T5[dx + 2, pl.ds(dy % ROWS, 1), :] = S5[dy + 2, pl.ds(gx + (dx + 2), 1), :]

    lane2 = lane // 2
    row_low, row_high = sub // 2, 4 + sub // 2

    wait_group(G_U2, n_u2)
    for i in range(5):
        low = take_rows(take_lanes(T5[i, 0:8], lane2), row_low)
        high = take_rows(take_lanes(T5[i, 8:16], lane2), row_high)
        for p in (2 * i, 2 * i + 1):
            v = U2[1, p] + jnp.concatenate([low, high], axis=0)
            M2[p:p + 1] = jnp.where(inside((1, ROWS, 128), p - 4, 2, 4), v[None], 0.0)
    sweep(at(M2, 4), 4, at(U2, 4, 0), C2, 3, to(VA2, 3), -3, 8, 4)
    sweep(at(VA2, 3), 3, at(U2, 4, 0), C2, 3, to(VB2, 2), -2, 6, 6)

    wait_group(G_V1, n_v1)
    for p1 in range(-3, 7):
        e = VB2[p1 // 2 + 2]
        good = inside((1, ROWS, 128), p1, 4, 3)
        for k in range(2):
            index = lane2 + 64 * k
            low = take_rows(take_lanes(e[0:8], index), row_low)
            high = take_rows(take_lanes(e[8:16], index), row_high)
            v = V1[k, p1 + 3] + jnp.concatenate([low, high], axis=0)
            M1[k, p1 + 3:p1 + 4] = jnp.where(good, v[None], 0.0)
    for k in range(2):
        sweep(at(M1, 3, k), 3, b1[k], C1, 2, to(VA1, 2, k), -2, 8, 4)
    sweep(at(VA1, 2, 0), 2, b1[0], C1, 2, to(VB1, 1, 0), -1, 6, 6)

    def store_coarse(p, n, x):
        coarse_ref[pl.ds(p, n)] = x[:, 0:4]

    sweep(at(VA1, 2, 1), 2, b1[1], C1, 2, store_coarse, 0, 4, 4, 8)

    wait_group(G_V0, n_v0)
    for p1 in range(-1, 5):
        e = VB1[0, p1 + 1]
        pieces = []
        for k in range(2):
            index = lane2 + 64 * k
            first, second = take_lanes(e[0:8], index), take_lanes(e[8:16], index)
            low = take_rows(first, row_low)
            high = jnp.where(sub < 4, take_rows(first, row_high), take_rows(second, row_high))
            pieces.append(jnp.concatenate([low, high], axis=0))
        e = jnp.concatenate(pieces, axis=1)
        v = V0[2 * p1 + 2:2 * p1 + 4] + e[None]
        VA0[2 * p1 + 2:2 * p1 + 4] = jnp.where(inside(v.shape, 2 * p1, 8, 2), v, 0.0)
    sweep(at(VA0, 2), 2, at(S0, 2), C0, 2, to(VB0, 1), -1, 10, 2)
    sweep(at(VB0, 1), 1, at(S0, 2), C0, 2, to(fine_ref, 0), 0, 8, 2, 8)

    for group, rows in ((G_K0, n_k0), (G_S0, n_s0), (G_E1, n_e1), (G_K2, n_k2), (G_ZK, n_zk), (G_GK, n_gk), (G_B1, n_b1),
                        (G_B2, n_b2), (G_ZB, n_zb), (G_GB, n_gb), (G_V0, n_v0), (G_V1, n_v1), (G_U2, n_u2)):
        wait_rows(rows, send_sem.at[group])


def solution(mesh):
    nx, ny = mesh.shape["gx"], mesh.shape["gy"]

    def vmem(*shape):
        return pltpu.VMEM(shape, F32)

    def on_device(source, kappa):
        scratch = [
            vmem(14, 16, 256), vmem(12, 16, 256), vmem(12, 16, 256), vmem(12, 16, 256), vmem(10, 16, 256),
            vmem(7, 13, 16, 256),
            vmem(2, 10, 16, 128), vmem(10, 16, 128), vmem(2, 10, 16, 128), vmem(2, 8, 16, 128), vmem(2, 6, 16, 128),
            vmem(7, 9, 16, 128), vmem(2, 10, 16, 128),
            vmem(10, 16, 128), vmem(6, 16, 128), vmem(2, 10, 16, 128), vmem(8, 16, 128), vmem(6, 16, 128),
            vmem(7, 9, 16, 128), vmem(10, 16, 128),
            vmem(16, 128), vmem(16, 128), vmem(ny, 8, 128), vmem(ny, 8, 128),
            vmem(7, ny, 8, 128), vmem(ny + 2, 8, 128), vmem(ny, 8, 128), vmem(ny, 8, 128), vmem(ny, 8, 128),
            vmem(ny + 4, 8, 128), vmem(5, 24, 128), vmem(5, 16, 128),
            vmem(512, 128),
            pltpu.SemaphoreType.DMA((2,)), pltpu.SemaphoreType.DMA((GROUPS,)), pltpu.SemaphoreType.DMA((GROUPS,)),
        ]
        return pl.pallas_call(
            lambda *refs: kernel(nx, ny, *refs),
            out_shape=(jax.ShapeDtypeStruct((8, 8, 256), F32), jax.ShapeDtypeStruct((4, 4, 128), F32)),
            in_specs=[pl.BlockSpec(memory_space=pl.ANY)] * 2,
            out_specs=[pl.BlockSpec(memory_space=pltpu.VMEM)] * 2,
            scratch_shapes=scratch,
            compiler_params=pltpu.CompilerParams(
                collective_id=0, has_side_effects=True, vmem_limit_bytes=32 * 1024 * 1024
            ),
            name="vcycles",
        )(source, kappa)

    spec = P("gx", "gy", None)
    return jax.shard_map(on_device, mesh=mesh, in_specs=(spec, spec), out_specs=(spec, spec), check_vma=False)
```

```python
import jax
import jax.numpy as jnp
from jax import lax
from jax.experimental import pallas as pl
from jax.experimental.pallas import tpu as pltpu
from jax.sharding import PartitionSpec as P


CSWEEPS = 8
OMEGA = 0.8
REACH = 4
F32 = jnp.float32
ROWS = 16

INNER = [(dx, dy) for dx in (-1, 1, 0) for dy in (0, -1, 1) if (dx, dy) != (0, 0)]
AROUND = INNER + [
    (dx, dy) for dx in (-2, 2, -1, 1, 0) for dy in (-2, -1, 0, 1, 2) if max(abs(dx), abs(dy)) == 2
]

(G_K0, G_S0, G_E1, G_K2, G_ZK, G_GK, G_B1, G_B2, G_ZB, G_GB, G_V0, G_V1, G_U2) = range(13)
GROUPS = 13


def span(step, size, rim):
    low = max(0, step * size - rim)
    high = min(size, size + rim + step * size)
    return low, high - low, low - step * size


def roll(x, shift, axis):
    return pltpu.roll(x, shift % x.shape[axis], axis)


def iota(shape, axis):
    return lax.broadcasted_iota(jnp.int32, shape, axis)


def take_lanes(x, index):
    return jnp.take_along_axis(x, index, axis=1)


def take_rows(x, index):
    return jnp.take_along_axis(x, index, axis=0)


def pair_lanes(a, b):
    lane = iota(a.shape, 1)
    index = lax.rem(2 * lane, 128)
    a = take_lanes(a + roll(a, -1, 1), index)
    if b is None:
        return a
    b = take_lanes(b + roll(b, -1, 1), index)
    return jnp.where(lane < 64, a, b)


def pair_rows(x):
    return take_rows(x + roll(x, -1, 0), lax.rem(2 * iota(x.shape, 0), 8))


def kernel(nx, ny, src_hbm, kap_hbm, fine_ref, coarse_ref, K0, S0, V0, VA0, VB0, C0, E1, B1, V1, VA1, VB1, C1, M1,
           K2, B2, U2, VA2, VB2, C2, M2, ZK, ZB, GK, GB, C3, R3, W3, P3, Q3, X3, S5, T5, D, local_sem, send_sem, recv_sem, word):
    gx = lax.axis_index("gx")
    gy = lax.axis_index("gy")
    mesh_ids = pl.DeviceIdType.MESH

    def peer(dx, dy):
        return (lax.rem(gx + (dx + nx), nx) if not isinstance(dx, int) or dx else gx,
                lax.rem(gy + (dy + ny), ny) if not isinstance(dy, int) or dy else gy)

    def wait_rows(rows, sem):
        pltpu.make_async_copy(D.at[pl.ds(0, rows)], D.at[pl.ds(0, rows)], sem).wait()

    def wait_group(group, rows):
        wait_rows(rows, recv_sem.at[group])

    def ship(group, ref, lead, steps, size, rim, corner, offset):
        total = 0
        for dx, dy in steps:
            reach = corner if dx and dy else rim
            px, cx, qx = span(dx, size, reach)
            py, cy, qy = span(dy, size, reach)
            here = (pl.ds(px + offset, cx), pl.ds(py, cy), slice(None))
            there = (pl.ds(qx + offset, cx), pl.ds(qy % ROWS, cy), slice(None))
            if lead is not None:
                here, there = (pl.ds(*lead),) + here, (pl.ds(*lead),) + there
            pltpu.make_async_remote_copy(
                src_ref=ref.at[here], dst_ref=ref.at[there], send_sem=send_sem.at[group], recv_sem=recv_sem.at[group],
                device_id=peer(dx, dy), device_id_type=mesh_ids,
            ).start()
            total += cx * cy * (ref.shape[-1] // 128) * (lead[1] if lead else 1)
        return total

    def ship_column(group, ref):
        def step(i, carry):
            pltpu.make_async_remote_copy(
                src_ref=ref.at[pl.ds(gx, 1)], dst_ref=ref.at[pl.ds(gx, 1)], send_sem=send_sem.at[group],
                recv_sem=recv_sem.at[group], device_id=(lax.rem(gx + i, nx), gy), device_id_type=mesh_ids,
            ).start()
            return carry
        lax.fori_loop(1, nx, step, 0)
        return nx - 1

    def ship_row(group, ref):
        def step(i, carry):
            pltpu.make_async_remote_copy(
                src_ref=ref.at[gy], dst_ref=ref.at[gy], send_sem=send_sem.at[group],
                recv_sem=recv_sem.at[group], device_id=(gx, lax.rem(gy + i, ny)), device_id_type=mesh_ids,
            ).start()
            return carry
        lax.fori_loop(1, ny, step, 0)
        return 8 * (ny - 1)

    copies = [
        pltpu.make_async_copy(kap_hbm, K0.at[pl.ds(3, 8), pl.ds(0, 8), :], local_sem.at[0]),
        pltpu.make_async_copy(src_hbm, S0.at[pl.ds(2, 8), pl.ds(0, 8), :], local_sem.at[1]),
    ]
    for copy in copies:
        copy.start()
    barrier = pltpu.get_barrier_semaphore()

    def greet(device):
        pl.semaphore_signal(barrier, inc=1, device_id=device, device_id_type=mesh_ids)

    def greet_y(i, carry):
        greet((gx, lax.rem(gy + i, ny)))
        return carry

    near = range(1, nx) if nx <= 2 * REACH else [*range(1, REACH + 1), *range(nx - REACH, nx)]
    corners = [(dx, dy) for dx, dy in INNER if dx and dy]
    for dx in near:
        greet(peer(dx, 0))
    for dx, dy in corners:
        greet(peer(dx, dy))
    lax.fori_loop(1, ny, greet_y, 0)
    pl.semaphore_wait(barrier, len(near) + ny - 1 + len(corners))
    for copy in copies:
        copy.wait()

    n_k0 = ship(G_K0, K0, None, INNER, 8, 3, 2, 3)
    n_s0 = ship(G_S0, S0, None, INNER, 8, 2, 1, 2)
    if nx > 2 * REACH:
        for dx in (REACH, -REACH):
            pl.semaphore_signal(word, inc=1, device_id=peer(dx, 0), device_id_type=mesh_ids)

    def restrict0(ref, offset, scale):
        out = []
        for i in range(4):
            both = ref[offset + 2 * i, 0:8, :] + ref[offset + 2 * i + 1, 0:8, :]
            out.append(scale * pair_rows(pair_lanes(both[:, :128], both[:, 128:])))
        return out

    own1 = restrict0(K0, 3, 0.125)
    for i, tile in enumerate(own1):
        E1[1, 3 + i, 0:4, :] = tile[0:4]
    for i, tile in enumerate(restrict0(S0, 2, 0.5)):
        E1[0, 3 + i, 0:4, :] = tile[0:4]
    n_e1 = ship(G_E1, E1, (0, 2), INNER, 4, 3, 3, 3)
    own2 = []
    for i in range(2):
        own2.append(0.125 * pair_rows(pair_lanes(own1[2 * i] + own1[2 * i + 1], None)))
        K2[4 + i, 0:2, :] = own2[i][0:2]
    both = own2[0] + own2[1]
    ZK[pl.ds(gx, 1), :] = 0.125 * pair_rows(pair_lanes(both, None))[0:1]

    def inside(shape, first, size, rim):
        plane = iota(shape, 0) + first + gx * size
        row = iota(shape, 1)
        row = jnp.where(row < 8 + size // 2, row, row - ROWS)
        good = (row >= -rim) & (row < size + rim)
        row = row + gy * size
        return good & (plane >= 0) & (plane < nx * size) & (row >= 0) & (row < ny * size)

    def faces(read, C, planes, width, depth, size, rim, first, chunk):
        for a in range(0, planes, chunk):
            n = min(chunk, planes - a)
            k = read(a, n + 2)
            mid = k[1:n + 1]
            west = 0.5 * (k[0:n + 1] + k[1:n + 2])
            C[0, a:a + n + 1] = west
            north = 0.5 * (mid + roll(mid, -1, 1))
            south = roll(north, 1, 1)
            z = lax.rem(iota(mid.shape, 2), depth)
            top = z == depth - 1
            bottom = z == 0
            above = 0.5 * (mid + jnp.where(top, 0.0, roll(mid, -1, 2)))
            below = 0.5 * (mid + jnp.where(bottom, 0.0, roll(mid, 1, 2)))
            total = west[0:n] + west[1:n + 1] + north + south + above + below
            C[1, a:a + n] = north
            C[2, a:a + n] = south
            C[3, a:a + n] = jnp.where(top, 0.0, above)
            C[4, a:a + n] = jnp.where(bottom, 0.0, below)
            C[5, a:a + n] = total
            C[6, a:a + n] = jnp.where(inside(mid.shape, first + a, size, rim), OMEGA / total, 0.0)

    def residual(v, b, C, c, n, rows=ROWS):
        mid = v[1:n + 1]
        cut = slice(0, rows)
        beside = C[0, c:c + n, cut] * v[0:n, cut] + C[0, c + 1:c + n + 1, cut] * v[2:n + 2, cut]
        beside += C[1, c:c + n, cut] * roll(mid, -1, 1)[:, cut] + C[2, c:c + n, cut] * roll(mid, 1, 1)[:, cut]
        mid = mid[:, cut]
        beside += C[3, c:c + n, cut] * roll(mid, -1, 2) + C[4, c:c + n, cut] * roll(mid, 1, 2)
        return b - C[5, c:c + n, cut] * mid + beside

    def sweep(V, vo, b, C, co, store, first, planes, chunk, rows=ROWS):
        for a in range(0, planes, chunk):
            n = min(chunk, planes - a)
            p = first + a
            v = V(p - 1, n + 2)
            r = residual(v, b(p, n, rows), C, p + co, n, rows)
            store(p, n, v[1:n + 1, 0:rows] + C[6, p + co:p + co + n, 0:rows] * r)

    wait_group(G_K0, n_k0)
    n_k2 = ship(G_K2, K2, None, AROUND, 2, 4, 4, 4)

    def read_k0(a, n):
        k = K0[a:a + n]
        return jnp.where(inside(k.shape, a - 3, 8, 3), k, 0.0)

    faces(read_k0, C0, 12, 256, 256, 8, 3, -2, 2)
    wait_group(G_S0, n_s0)
    for a in range(0, 12, 2):
        VA0[a:a + 2] = C0[6, a:a + 2] * S0[a:a + 2]

    def at(ref, offset, lead=None):
        def read(p, n, rows=ROWS):
            where = (pl.ds(p + offset, n), pl.ds(0, rows), slice(None))
            return ref[where] if lead is None else ref[(lead,) + where]
        return read

    def to(ref, offset, lead=None):
        def store(p, n, x):
            where = (pl.ds(p + offset, n), pl.ds(0, x.shape[1]), slice(None))
            if lead is None:
                ref[where] = x
            else:
                ref[(lead,) + where] = x
        return store

    sweep(at(VA0, 2), 2, at(S0, 2), C0, 2, to(VB0, 1), -1, 10, 2)
    for i in range(4):
        r = residual(VB0[2 * i:2 * i + 4], S0[2 + 2 * i:4 + 2 * i, 0:8], C0, 2 + 2 * i, 2, 8)
        both = r[0] + r[1]
        B1[3 + i, 0:4, :] = 0.5 * pair_rows(pair_lanes(both[:, :128], both[:, 128:]))[0:4]
    n_b1 = ship(G_B1, B1, None, INNER, 4, 2, 2, 3)
    if nx > 2 * REACH:
        pl.semaphore_wait(word, 2)
    n_zk = ship_column(G_ZK, ZK)
    V0[2:10, 0:8, :] = VB0[1:9, 0:8, :]


    def packed(ref):
        keep = lax.rem(iota((8, 128), 0) + 8 * (iota((8, 128), 1) // 64), 16) < nx
        return jnp.where(keep, jnp.where(iota((8, 128), 1) < 64, ref[0:8], ref[8:16]), 0.0)

    wait_group(G_E1, n_e1)

    def read_k1(a, n):
        k = E1[1, a:a + n]
        return jnp.where(inside(k.shape, a - 3, 4, 3), k, 0.0)

    faces(read_k1, C1, 8, 128, 128, 4, 3, -2, 4)
    b1 = (at(B1, 3), at(E1, 3, 0))

    def down1(k):
        for a in range(0, 8, 4):
            VA1[k, a:a + 4] = C1[6, a:a + 4] * b1[k](a - 2, 4)
        sweep(at(VA1, 2, k), 2, b1[k], C1, 2, to(VB1, 1, k), -1, 6, 6)
        r = residual(VB1[k], b1[k](0, 4, 8), C1, 2, 4, 8)
        V1[k, 3:7, 0:4, :] = VB1[k, 1:5, 0:4, :]
        return r[0] + r[1], r[2] + r[3]

    pairs_c = down1(1)
    wait_group(G_B1, n_b1)
    pairs_f = down1(0)
    for i in range(2):
        tile = 0.5 * pair_rows(pair_lanes(pairs_f[i], pairs_c[i]))
        B2[2 + i, 0:2, :] = tile[0:2]
        U2[0, 4 + i, 0:2, :] = tile[0:2]
    n_b2 = ship(G_B2, B2, None, INNER, 2, 2, 2, 2)
    wait_group(G_ZK, n_zk)
    GK[gy] = packed(ZK)
    n_gk = ship_row(G_GK, GK)

    wait_group(G_K2, n_k2)

    def read_k2(a, n):
        k = K2[a:a + n]
        return jnp.where(inside(k.shape, a - 4, 2, 4), k, 0.0)

    faces(read_k2, C2, 8, 128, 64, 2, 4, -3, 4)
    wait_group(G_B2, n_b2)
    VA2[0:6] = C2[6, 1:7] * B2[0:6]
    sweep(at(VA2, 2), 2, at(B2, 2), C2, 3, to(VB2, 1), -1, 4, 4)
    r = residual(VB2[0:4], B2[2:4, 0:8], C2, 3, 2, 8)
    U2[1, 4:6, 0:2, :] = VB2[1:3, 0:2, :]
    ZB[pl.ds(gx, 1), :] = 0.5 * pair_rows(pair_lanes(r[0] + r[1], None))[0:1]
    n_zb = ship_column(G_ZB, ZB)

    shape = (8, 128)
    sub, lane = iota(shape, 0), iota(shape, 1)
    half = lane // 64
    at_x = sub + 8 * half
    z = lax.rem(lane, 32)
    first_rhs = lax.rem(lane, 64) < 32

    def next_x(v):
        a = roll(v, -1, 1)
        return jnp.where(sub == 7, roll(a, 64, 2), a)

    def previous_x(v):
        a = roll(v, 1, 1)
        return jnp.where(sub == 0, roll(a, 64, 2), a)

    wait_group(G_GK, n_gk)
    chunk3 = min(8, ny)
    blank = jnp.zeros(shape, F32)
    for a in range(0, ny, chunk3):
        k = GK[a:a + chunk3]
        up_y = [GK[j] if j < ny else blank for j in range(a + 1, a + chunk3 + 1)]
        down_y = [GK[j] if j >= 0 else blank for j in range(a - 1, a + chunk3 - 1)]
        y_next = 0.5 * (k + jnp.stack(up_y))
        y_previous = 0.5 * (k + jnp.stack(down_y))
        x_next = 0.5 * (k + jnp.where(at_x < nx - 1, next_x(k), 0.0))
        x_previous = 0.5 * (k + jnp.where(at_x > 0, previous_x(k), 0.0))
        z_next = 0.5 * (k + jnp.where(z < 31, roll(k, -1, 2), 0.0))
        z_previous = 0.5 * (k + jnp.where(z > 0, roll(k, 1, 2), 0.0))
        C3[0, a:a + chunk3] = y_previous
        C3[1, a:a + chunk3] = y_next
        C3[2, a:a + chunk3] = jnp.where(at_x < nx - 1, x_next, 0.0)
        C3[3, a:a + chunk3] = jnp.where((at_x > 0) & (at_x < nx), x_previous, 0.0)
        C3[4, a:a + chunk3] = jnp.where(z < 31, z_next, 0.0)
        C3[5, a:a + chunk3] = jnp.where(z > 0, z_previous, 0.0)
        C3[6, a:a + chunk3] = y_next + y_previous + x_next + x_previous + z_next + z_previous
    R3[0] = blank
    R3[ny + 1] = blank

    wait_group(G_ZB, n_zb)
    GB[gy] = packed(ZB)
    n_gb = ship_row(G_GB, GB)
    n_v0 = ship(G_V0, V0, None, INNER, 8, 2, 1, 2)
    n_v1 = ship(G_V1, V1, (0, 2), INNER, 4, 3, 3, 3)
    n_u2 = ship(G_U2, U2, (0, 2), AROUND, 2, 4, 4, 4)
    for a in range(0, ny, chunk3):
        P3[a:a + chunk3] = jnp.zeros((chunk3,) + shape, F32)
        Q3[a:a + chunk3] = jnp.zeros((chunk3,) + shape, F32)
        X3[2 + a:2 + a + chunk3] = jnp.zeros((chunk3,) + shape, F32)
    wait_group(G_GB, n_gb)
    for a in range(0, ny, chunk3):
        R3[1 + a:1 + a + chunk3] = GB[a:a + chunk3]

    def over_grid(x):
        x = jnp.sum(x, axis=0, keepdims=True)
        first = jnp.sum(jnp.where(first_rhs[0:1], x, 0.0), axis=1, keepdims=True)
        second = jnp.sum(jnp.where(first_rhs[0:1], 0.0, x), axis=1, keepdims=True)
        return jnp.where(first_rhs[0:1], first, second)

    def iteration(_, carry):
        norm_before, alpha_before = carry
        norm, energy = blank, blank
        for a in range(0, ny, chunk3):
            mid = R3[1 + a:1 + a + chunk3]
            beside = C3[0, a:a + chunk3] * R3[a:a + chunk3] + C3[1, a:a + chunk3] * R3[2 + a:2 + a + chunk3]
            beside += C3[2, a:a + chunk3] * next_x(mid) + C3[3, a:a + chunk3] * previous_x(mid)
            beside += C3[4, a:a + chunk3] * roll(mid, -1, 2) + C3[5, a:a + chunk3] * roll(mid, 1, 2)
            image = C3[6, a:a + chunk3] * mid - beside
            W3[a:a + chunk3] = image
            norm += jnp.sum(mid * mid, axis=0)
            energy += jnp.sum(mid * image, axis=0)
        norm, energy = over_grid(norm), over_grid(energy)
        beta = norm / norm_before
        alpha = norm / (energy - beta * norm / alpha_before)
        for a in range(0, ny, chunk3):
            p = R3[1 + a:1 + a + chunk3] + beta * P3[a:a + chunk3]
            q = W3[a:a + chunk3] + beta * Q3[a:a + chunk3]
            P3[a:a + chunk3] = p
            Q3[a:a + chunk3] = q
            X3[2 + a:2 + a + chunk3] += alpha * p
            R3[1 + a:1 + a + chunk3] -= alpha * q
        return norm, alpha

    lax.fori_loop(0, CSWEEPS, iteration, (jnp.full((1, 128), jnp.inf, F32), jnp.ones((1, 128), F32)))

    near = X3[pl.ds(gy, 5)]
    S5[:, 2:10, :] = near
    S5[:, 10:18, :] = roll(near, 64, 2)
    for dx in range(-2, 3):
        for dy in range(-2, 3):
            T5[dx + 2, pl.ds(dy % ROWS, 1), :] = S5[dy + 2, pl.ds(gx + (dx + 2), 1), :]

    lane2 = lane // 2
    row_low, row_high = sub // 2, 4 + sub // 2

    wait_group(G_U2, n_u2)
    for i in range(5):
        low = take_rows(take_lanes(T5[i, 0:8], lane2), row_low)
        high = take_rows(take_lanes(T5[i, 8:16], lane2), row_high)
        for p in (2 * i, 2 * i + 1):
            v = U2[1, p] + jnp.concatenate([low, high], axis=0)
            M2[p:p + 1] = jnp.where(inside((1, ROWS, 128), p - 4, 2, 4), v[None], 0.0)
    sweep(at(M2, 4), 4, at(U2, 4, 0), C2, 3, to(VA2, 3), -3, 8, 4)
    sweep(at(VA2, 3), 3, at(U2, 4, 0), C2, 3, to(VB2, 2), -2, 6, 6)

    wait_group(G_V1, n_v1)
    for p1 in range(-3, 7):
        e = VB2[p1 // 2 + 2]
        good = inside((1, ROWS, 128), p1, 4, 3)
        for k in range(2):
            index = lane2 + 64 * k
            low = take_rows(take_lanes(e[0:8], index), row_low)
            high = take_rows(take_lanes(e[8:16], index), row_high)
            v = V1[k, p1 + 3] + jnp.concatenate([low, high], axis=0)
            M1[k, p1 + 3:p1 + 4] = jnp.where(good, v[None], 0.0)
    for k in range(2):
        sweep(at(M1, 3, k), 3, b1[k], C1, 2, to(VA1, 2, k), -2, 8, 4)
    sweep(at(VA1, 2, 0), 2, b1[0], C1, 2, to(VB1, 1, 0), -1, 6, 6)

    def store_coarse(p, n, x):
        coarse_ref[pl.ds(p, n)] = x[:, 0:4]

    sweep(at(VA1, 2, 1), 2, b1[1], C1, 2, store_coarse, 0, 4, 4, 8)

    wait_group(G_V0, n_v0)
    for p1 in range(-1, 5):
        e = VB1[0, p1 + 1]
        pieces = []
        for k in range(2):
            index = lane2 + 64 * k
            first, second = take_lanes(e[0:8], index), take_lanes(e[8:16], index)
            low = take_rows(first, row_low)
            high = jnp.where(sub < 4, take_rows(first, row_high), take_rows(second, row_high))
            pieces.append(jnp.concatenate([low, high], axis=0))
        e = jnp.concatenate(pieces, axis=1)
        v = V0[2 * p1 + 2:2 * p1 + 4] + e[None]
        VA0[2 * p1 + 2:2 * p1 + 4] = jnp.where(inside(v.shape, 2 * p1, 8, 2), v, 0.0)
    sweep(at(VA0, 2), 2, at(S0, 2), C0, 2, to(VB0, 1), -1, 10, 2)
    sweep(at(VB0, 1), 1, at(S0, 2), C0, 2, to(fine_ref, 0), 0, 8, 2, 8)

    for group, rows in ((G_K0, n_k0), (G_S0, n_s0), (G_E1, n_e1), (G_K2, n_k2), (G_ZK, n_zk), (G_GK, n_gk), (G_B1, n_b1),
                        (G_B2, n_b2), (G_ZB, n_zb), (G_GB, n_gb), (G_V0, n_v0), (G_V1, n_v1), (G_U2, n_u2)):
        wait_rows(rows, send_sem.at[group])


def put_out(fine, coarse, fine_out, coarse_out, sem):
    copies = [
        pltpu.make_async_copy(fine, fine_out, sem.at[0]),
        pltpu.make_async_copy(coarse, coarse_out, sem.at[1]),
    ]
    for copy in copies:
        copy.start()
    for copy in copies:
        copy.wait()


def solution(mesh):
    nx, ny = mesh.shape["gx"], mesh.shape["gy"]

    def vmem(*shape):
        return pltpu.VMEM(shape, F32)

    def on_device(source, kappa):
        scratch = [
            vmem(14, 16, 256), vmem(12, 16, 256), vmem(12, 16, 256), vmem(12, 16, 256), vmem(10, 16, 256),
            vmem(7, 13, 16, 256),
            vmem(2, 10, 16, 128), vmem(10, 16, 128), vmem(2, 10, 16, 128), vmem(2, 8, 16, 128), vmem(2, 6, 16, 128),
            vmem(7, 9, 16, 128), vmem(2, 10, 16, 128),
            vmem(10, 16, 128), vmem(6, 16, 128), vmem(2, 10, 16, 128), vmem(8, 16, 128), vmem(6, 16, 128),
            vmem(7, 9, 16, 128), vmem(10, 16, 128),
            vmem(16, 128), vmem(16, 128), vmem(ny, 8, 128), vmem(ny, 8, 128),
            vmem(7, ny, 8, 128), vmem(ny + 2, 8, 128), vmem(ny, 8, 128), vmem(ny, 8, 128), vmem(ny, 8, 128),
            vmem(ny + 4, 8, 128), vmem(5, 24, 128), vmem(5, 16, 128),
            vmem(512, 128),
            pltpu.SemaphoreType.DMA((2,)), pltpu.SemaphoreType.DMA((GROUPS,)), pltpu.SemaphoreType.DMA((GROUPS,)), pltpu.SemaphoreType.REGULAR,
        ]
        fine, coarse = pl.pallas_call(
            lambda *refs: kernel(nx, ny, *refs),
            out_shape=(jax.ShapeDtypeStruct((8, 8, 256), F32), jax.ShapeDtypeStruct((4, 4, 128), F32)),
            in_specs=[pl.BlockSpec(memory_space=pltpu.HBM)] * 2,
            out_specs=[pl.BlockSpec(memory_space=pltpu.VMEM)] * 2,
            scratch_shapes=scratch,
            compiler_params=pltpu.CompilerParams(
                collective_id=0, has_side_effects=True, vmem_limit_bytes=32 * 1024 * 1024
            ),
            name="vcycles",
        )(*(pltpu.with_memory_space_constraint(x, pltpu.HBM) for x in (source, kappa)))
        return pl.pallas_call(
            put_out,
            out_shape=(jax.ShapeDtypeStruct((8, 8, 256), F32), jax.ShapeDtypeStruct((4, 4, 128), F32)),
            in_specs=[pl.BlockSpec(memory_space=pltpu.VMEM)] * 2,
            out_specs=[pl.BlockSpec(memory_space=pltpu.HBM)] * 2,
            scratch_shapes=[pltpu.SemaphoreType.DMA((2,))],
            name="put_out",
        )(fine, coarse)

    spec = P("gx", "gy", None)
    return jax.shard_map(on_device, mesh=mesh, in_specs=(spec, spec), out_specs=(spec, spec), check_vma=False)
```

```python
import jax
import jax.numpy as jnp
from jax import lax
from jax.experimental import pallas as pl
from jax.experimental.pallas import tpu as pltpu
from jax.sharding import PartitionSpec as P


CSWEEPS = 8
OMEGA = 0.8
REACH = 4
F32 = jnp.float32
ROWS = 16

INNER = [(-1, -1), (-1, 1), (1, -1), (1, 1), (-1, 0), (1, 0), (0, -1), (0, 1)]
AROUND = INNER + [
    (dx, dy) for dx in (-2, 2, -1, 1, 0) for dy in (-2, -1, 0, 1, 2) if max(abs(dx), abs(dy)) == 2
]

(G_K0, G_S0, G_E1, G_K2, G_KC, G_GK, G_B1, G_BF, G_BC, G_GB, G_V0, G_V1, G_U2, G_KD) = range(14)
GROUPS = 14


def span(step, size, rim):
    low = max(0, step * size - rim)
    high = min(size, size + rim + step * size)
    return low, high - low, low - step * size


def roll(x, shift, axis):
    return pltpu.roll(x, shift % x.shape[axis], axis)


def iota(shape, axis):
    return lax.broadcasted_iota(jnp.int32, shape, axis)


def take_lanes(x, index):
    return jnp.take_along_axis(x, index, axis=1)


def take_rows(x, index):
    return jnp.take_along_axis(x, index, axis=0)


def pair_lanes(a, b):
    lane = iota(a.shape, 1)
    index = lax.rem(2 * lane, 128)
    a = take_lanes(a + roll(a, -1, 1), index)
    if b is None:
        return a
    b = take_lanes(b + roll(b, -1, 1), index)
    return jnp.where(lane < 64, a, b)


def pair_rows(x):
    return take_rows(x + roll(x, -1, 0), lax.rem(2 * iota(x.shape, 0), 8))


def kernel(nx, ny, src_hbm, kap_hbm, fine_ref, coarse_ref, K0, S0, V0, VA0, VB0, C0, E1, B1, V1, VA1, VB1, C1, M1,
           K2, U2, VA2, VB2, C2, M2, KC, BF, BC, KM, VC, WC, PF, PC, CC, ZK, ZB, GK, GB, C3, R3, W3, P3, Q3, X3, S5, T5, D, local_sem, send_sem, recv_sem, word):
    gx = lax.axis_index("gx")
    gy = lax.axis_index("gy")
    mesh_ids = pl.DeviceIdType.MESH

    def peer(dx, dy):
        return (lax.rem(gx + (dx + nx), nx) if not isinstance(dx, int) or dx else gx,
                lax.rem(gy + (dy + ny), ny) if not isinstance(dy, int) or dy else gy)

    def wait_rows(rows, sem):
        pltpu.make_async_copy(D.at[pl.ds(0, rows)], D.at[pl.ds(0, rows)], sem).wait()

    def wait_group(group, rows):
        wait_rows(rows, recv_sem.at[group])

    def ship(group, ref, lead, steps, size, rim, corner, offset):
        total = 0
        for dx, dy in steps:
            reach = corner if dx and dy else rim
            px, cx, qx = span(dx, size, reach)
            py, cy, qy = span(dy, size, reach)
            here = (pl.ds(px + offset, cx), pl.ds(py, cy), slice(None))
            there = (pl.ds(qx + offset, cx), pl.ds(qy % ROWS, cy), slice(None))
            if lead is not None:
                here, there = (pl.ds(*lead),) + here, (pl.ds(*lead),) + there
            pltpu.make_async_remote_copy(
                src_ref=ref.at[here], dst_ref=ref.at[there], send_sem=send_sem.at[group], recv_sem=recv_sem.at[group],
                device_id=peer(dx, dy), device_id_type=mesh_ids,
            ).start()
            total += cx * cy * (ref.shape[-1] // 128) * (lead[1] if lead else 1)
        return total

    pieces = {0: (0, 2, 0), -1: (0, 2, 2), 1: (0, 2, 6), -2: (0, 1, 4), 2: (1, 1, 5)}

    def ship_sides(group, ref):
        total = 0
        for dy in (-2, 2, -1, 1):
            here, count, there = pieces[dy]
            pltpu.make_async_remote_copy(
                src_ref=ref.at[:, pl.ds(here, count), :], dst_ref=ref.at[:, pl.ds(there, count), :],
                send_sem=send_sem.at[group], recv_sem=recv_sem.at[group],
                device_id=peer(0, dy), device_id_type=mesh_ids,
            ).start()
            total += nx * count
        return total

    def ship_columns(group, ref, spread):
        def pass_on(x, steps):
            for dy in steps:
                here, count, there = pieces[dy]
                pltpu.make_async_remote_copy(
                    src_ref=ref.at[pl.ds(gx, 1), pl.ds(here, count), :], dst_ref=ref.at[pl.ds(gx, 1), pl.ds(there, count), :],
                    send_sem=send_sem.at[group], recv_sem=recv_sem.at[group],
                    device_id=(x, peer(0, dy)[1]), device_id_type=mesh_ids,
                ).start()

        sides = [dy for dy in (-2, 2, -1, 1) if abs(dy) <= spread]

        def step(i, carry):
            far = nx // 2 + (1 - 2 * lax.rem(i, 2)) * ((i + 1) // 2)
            pass_on(lax.rem(gx + far, nx), sides + [0])
            return carry

        lax.fori_loop(0, nx - 1, step, 0)
        pass_on(gx, sides)
        return 2 * (nx - 1) + nx * sum(pieces[dy][1] for dy in sides)

    def ship_row(group, ref):
        def step(i, carry):
            pltpu.make_async_remote_copy(
                src_ref=ref.at[gy], dst_ref=ref.at[gy], send_sem=send_sem.at[group],
                recv_sem=recv_sem.at[group], device_id=(gx, lax.rem(gy + i, ny)), device_id_type=mesh_ids,
            ).start()
            return carry
        lax.fori_loop(1, ny, step, 0)
        return 8 * (ny - 1)

    copies = [
        pltpu.make_async_copy(kap_hbm, K0.at[pl.ds(3, 8), pl.ds(0, 8), :], local_sem.at[0]),
        pltpu.make_async_copy(src_hbm, S0.at[pl.ds(2, 8), pl.ds(0, 8), :], local_sem.at[1]),
    ]
    for copy in copies:
        copy.start()
    barrier = pltpu.get_barrier_semaphore()

    def greet(device):
        pl.semaphore_signal(barrier, inc=1, device_id=device, device_id_type=mesh_ids)

    def greet_y(i, carry):
        greet((gx, lax.rem(gy + i, ny)))
        return carry

    near = range(1, nx) if nx <= 2 * REACH else [*range(1, REACH + 1), *range(nx - REACH, nx)]
    corners = [(dx, dy) for dx, dy in INNER if dx and dy]
    for dx in near:
        greet(peer(dx, 0))
    for dx, dy in corners:
        greet(peer(dx, dy))
    lax.fori_loop(1, ny, greet_y, 0)
    pl.semaphore_wait(barrier, len(near) + ny - 1 + len(corners))
    for copy in copies:
        copy.wait()

    n_k0 = ship(G_K0, K0, None, INNER, 8, 3, 2, 3)
    n_s0 = ship(G_S0, S0, None, INNER, 8, 2, 1, 2)
    if nx > 2 * REACH:
        for dx in (REACH, -REACH):
            pl.semaphore_signal(word.at[0], inc=1, device_id=peer(dx, 0), device_id_type=mesh_ids)

    def restrict0(ref, offset, scale):
        out = []
        for i in range(4):
            both = ref[offset + 2 * i, 0:8, :] + ref[offset + 2 * i + 1, 0:8, :]
            out.append(scale * pair_rows(pair_lanes(both[:, :128], both[:, 128:])))
        return out

    own1 = restrict0(K0, 3, 0.125)
    for i, tile in enumerate(own1):
        E1[1, 3 + i, 0:4, :] = tile[0:4]
    for i, tile in enumerate(restrict0(S0, 2, 0.5)):
        E1[0, 3 + i, 0:4, :] = tile[0:4]
    n_e1 = ship(G_E1, E1, (0, 2), INNER, 4, 3, 3, 3)
    own2 = []
    for i in range(2):
        own2.append(0.125 * pair_rows(pair_lanes(own1[2 * i] + own1[2 * i + 1], None)))
        K2[4 + i, 0:2, :] = own2[i][0:2]
    KC[pl.ds(gx, 1), 0:2, :] = jnp.where(iota((8, 128), 1) < 64, own2[0], own2[1])[None, 0:2]

    def inside(shape, first, size, rim):
        plane = iota(shape, 0) + first + gx * size
        row = iota(shape, 1)
        row = jnp.where(row < 8 + size // 2, row, row - ROWS)
        good = (row >= -rim) & (row < size + rim)
        row = row + gy * size
        return good & (plane >= 0) & (plane < nx * size) & (row >= 0) & (row < ny * size)

    def faces(read, C, planes, width, depth, size, rim, first, chunk):
        for a in range(0, planes, chunk):
            n = min(chunk, planes - a)
            k = read(a, n + 2)
            mid = k[1:n + 1]
            west = 0.5 * (k[0:n + 1] + k[1:n + 2])
            C[0, a:a + n + 1] = west
            north = 0.5 * (mid + roll(mid, -1, 1))
            south = roll(north, 1, 1)
            z = lax.rem(iota(mid.shape, 2), depth)
            top = z == depth - 1
            bottom = z == 0
            above = 0.5 * (mid + jnp.where(top, 0.0, roll(mid, -1, 2)))
            below = 0.5 * (mid + jnp.where(bottom, 0.0, roll(mid, 1, 2)))
            total = west[0:n] + west[1:n + 1] + north + south + above + below
            C[1, a:a + n] = north
            C[2, a:a + n] = south
            C[3, a:a + n] = jnp.where(top, 0.0, above)
            C[4, a:a + n] = jnp.where(bottom, 0.0, below)
            C[5, a:a + n] = total
            C[6, a:a + n] = jnp.where(inside(mid.shape, first + a, size, rim), OMEGA / total, 0.0)

    def residual(v, b, C, c, n, rows=ROWS):
        mid = v[1:n + 1]
        cut = slice(0, rows)
        beside = C[0, c:c + n, cut] * v[0:n, cut] + C[0, c + 1:c + n + 1, cut] * v[2:n + 2, cut]
        beside += C[1, c:c + n, cut] * roll(mid, -1, 1)[:, cut] + C[2, c:c + n, cut] * roll(mid, 1, 1)[:, cut]
        mid = mid[:, cut]
        beside += C[3, c:c + n, cut] * roll(mid, -1, 2) + C[4, c:c + n, cut] * roll(mid, 1, 2)
        return b - C[5, c:c + n, cut] * mid + beside

    def sweep(V, vo, b, C, co, store, first, planes, chunk, rows=ROWS):
        for a in range(0, planes, chunk):
            n = min(chunk, planes - a)
            p = first + a
            v = V(p - 1, n + 2)
            r = residual(v, b(p, n, rows), C, p + co, n, rows)
            store(p, n, v[1:n + 1, 0:rows] + C[6, p + co:p + co + n, 0:rows] * r)

    wait_group(G_K0, n_k0)
    n_k2 = ship(G_K2, K2, None, AROUND, 2, 4, 4, 4)
    if nx > 2 * REACH:
        pl.semaphore_wait(word.at[0], 2)
    for dy in (-1, 1):
        pl.semaphore_signal(word.at[1], inc=1, device_id=peer(0, dy), device_id_type=mesh_ids)

    def read_k0(a, n):
        k = K0[a:a + n]
        return jnp.where(inside(k.shape, a - 3, 8, 3), k, 0.0)

    faces(read_k0, C0, 12, 256, 256, 8, 3, -2, 2)
    wait_group(G_S0, n_s0)
    for a in range(0, 12, 2):
        VA0[a:a + 2] = C0[6, a:a + 2] * S0[a:a + 2]

    def at(ref, offset, lead=None):
        def read(p, n, rows=ROWS):
            where = (pl.ds(p + offset, n), pl.ds(0, rows), slice(None))
            return ref[where] if lead is None else ref[(lead,) + where]
        return read

    def to(ref, offset, lead=None):
        def store(p, n, x):
            where = (pl.ds(p + offset, n), pl.ds(0, x.shape[1]), slice(None))
            if lead is None:
                ref[where] = x
            else:
                ref[(lead,) + where] = x
        return store

    sweep(at(VA0, 2), 2, at(S0, 2), C0, 2, to(VB0, 1), -1, 10, 2)
    for i in range(4):
        r = residual(VB0[2 * i:2 * i + 4], S0[2 + 2 * i:4 + 2 * i, 0:8], C0, 2 + 2 * i, 2, 8)
        both = r[0] + r[1]
        B1[3 + i, 0:4, :] = 0.5 * pair_rows(pair_lanes(both[:, :128], both[:, 128:]))[0:4]
    n_b1 = ship(G_B1, B1, None, INNER, 4, 2, 2, 3)
    n_kc = ship_columns(G_KC, KC, 0)
    V0[2:10, 0:8, :] = VB0[1:9, 0:8, :]


    def packed(ref):
        keep = lax.rem(iota((8, 128), 0) + 8 * (iota((8, 128), 1) // 64), 16) < nx
        return jnp.where(keep, jnp.where(iota((8, 128), 1) < 64, ref[0:8], ref[8:16]), 0.0)

    wait_group(G_E1, n_e1)

    def read_k1(a, n):
        k = E1[1, a:a + n]
        return jnp.where(inside(k.shape, a - 3, 4, 3), k, 0.0)

    faces(read_k1, C1, 8, 128, 128, 4, 3, -2, 4)
    b1 = (at(B1, 3), at(E1, 3, 0))

    def down1(k):
        for a in range(0, 8, 4):
            VA1[k, a:a + 4] = C1[6, a:a + 4] * b1[k](a - 2, 4)
        sweep(at(VA1, 2, k), 2, b1[k], C1, 2, to(VB1, 1, k), -1, 6, 6)
        r = residual(VB1[k], b1[k](0, 4, 8), C1, 2, 4, 8)
        V1[k, 3:7, 0:4, :] = VB1[k, 1:5, 0:4, :]
        return r[0] + r[1], r[2] + r[3]

    lane = iota((8, 128), 1)
    sub = iota((8, 128), 0)

    def right2(pairs, ref):
        tiles = [0.5 * pair_rows(pair_lanes(x, None)) for x in pairs]
        ref[pl.ds(gx, 1), 0:2, :] = jnp.where(lane < 64, tiles[0], tiles[1])[None, 0:2]
        return tiles

    tiles_c = right2(down1(1), BC)
    pl.semaphore_wait(word.at[1], 2)
    n_bc = ship_columns(G_BC, BC, 1)
    wait_group(G_B1, n_b1)
    tiles_f = right2(down1(0), BF)
    n_bf = ship_columns(G_BF, BF, 1)
    for i in range(2):
        U2[0, 4 + i, 0:2, :] = jnp.where(lane < 64, tiles_f[i], tiles_c[i])[0:2]

    even = lane < 64
    deep = lax.rem(lane, 64)
    row = jnp.where(sub < 5, sub, sub - 8) + 2 * gy
    good2 = (row >= 0) & (row < 2 * ny)
    blank = jnp.zeros((8, 128), F32)
    chunk2 = min(8, nx)
    for ref in (KM, VC, WC):
        ref[0] = blank
        ref[nx + 1] = blank

    def beside_x(v):
        n = v.shape[0] - 2
        v = roll(v, 64, 2)
        return jnp.where(even, v[0:n], v[1:n + 1]), jnp.where(even, v[1:n + 1], v[2:n + 2])

    wait_group(G_KC, n_kc)
    n_kd = ship_sides(G_KD, KC)
    wait_group(G_K2, n_k2)

    def read_k2(a, n):
        k = K2[a:a + n]
        return jnp.where(inside(k.shape, a - 4, 2, 4), k, 0.0)

    faces(read_k2, C2, 8, 128, 64, 2, 4, -3, 4)
    wait_group(G_KD, n_kd)
    for i in range(nx):
        KM[1 + i] = jnp.where(good2, KC[i], 0.0)
    for a in range(0, nx, chunk2):
        k = KM[a:a + chunk2 + 2]
        mid = k[1:chunk2 + 1]
        previous, following = beside_x(k)
        west, east = 0.5 * (mid + previous), 0.5 * (mid + following)
        north = 0.5 * (mid + roll(mid, -1, 1))
        south = roll(north, 1, 1)
        above = 0.5 * (mid + jnp.where(deep == 63, 0.0, roll(mid, -1, 2)))
        below = 0.5 * (mid + jnp.where(deep == 0, 0.0, roll(mid, 1, 2)))
        total = west + east + north + south + above + below
        CC[0, a:a + chunk2] = west
        CC[1, a:a + chunk2] = east
        CC[2, a:a + chunk2] = north
        CC[3, a:a + chunk2] = south
        CC[4, a:a + chunk2] = jnp.where(deep == 63, 0.0, above)
        CC[5, a:a + chunk2] = jnp.where(deep == 0, 0.0, below)
        CC[6, a:a + chunk2] = total
        CC[7, a:a + chunk2] = jnp.where(good2, OMEGA / total, 0.0)

    def pooled(tile):
        tile = tile + roll(tile, 64, 1)
        return tile + roll(tile, -1, 0)

    for i in range(nx):
        ZK[i:i + 1, :] = 0.125 * pair_lanes(pooled(KM[1 + i]), None)[0:1]

    def packed(ref):
        keep = sub + 8 * (lane // 64) < nx
        return jnp.where(keep, jnp.where(lane < 64, ref[0:8], ref[8:16]), 0.0)

    GK[gy] = packed(ZK)
    n_gk = ship_row(G_GK, GK)

    def residual2(V, b, a, n):
        v = V[a:a + n + 2]
        mid = v[1:n + 1]
        previous, following = beside_x(v)
        c = [CC[j, a:a + n] for j in range(7)]
        beside = c[0] * previous + c[1] * following + c[2] * roll(mid, -1, 1) + c[3] * roll(mid, 1, 1)
        beside += c[4] * roll(mid, -1, 2) + c[5] * roll(mid, 1, 2)
        return b[a:a + n] - c[6] * mid + beside

    def down2(b, summed):
        for a in range(0, nx, chunk2):
            VC[1 + a:1 + a + chunk2] = CC[7, a:a + chunk2] * b[a:a + chunk2]
        for a in range(0, nx, chunk2):
            v = VC[1 + a:1 + a + chunk2] + CC[7, a:a + chunk2] * residual2(VC, b, a, chunk2)
            WC[1 + a:1 + a + chunk2] = v
        own = WC[pl.ds(1 + gx, 1)][0]
        for a in range(0, nx, chunk2):
            r = residual2(WC, b, a, chunk2)
            for i in range(chunk2):
                summed[a + i] = pooled(r[i])
        return own

    wait_group(G_BC, n_bc)
    own_c = down2(BC, PC)

    shape = (8, 128)
    half = lane // 64
    at_x = sub + 8 * half
    z = lax.rem(lane, 32)
    first_rhs = lax.rem(lane, 64) < 32

    def next_x(v):
        a = roll(v, -1, 1)
        return jnp.where(sub == 7, roll(a, 64, 2), a)

    def previous_x(v):
        a = roll(v, 1, 1)
        return jnp.where(sub == 0, roll(a, 64, 2), a)

    wait_group(G_BF, n_bf)
    own_f = down2(BF, PF)
    for i in range(nx):
        ZB[i:i + 1, :] = 0.5 * pair_lanes(jnp.where(even, PF[i], PC[i]), None)[0:1]
    GB[gy] = packed(ZB)
    n_gb = ship_row(G_GB, GB)
    U2[1, 4, 0:2, :] = jnp.where(even, own_f, roll(own_c, 64, 1))[0:2]
    U2[1, 5, 0:2, :] = jnp.where(even, roll(own_f, 64, 1), own_c)[0:2]
    n_v0 = ship(G_V0, V0, None, INNER, 8, 2, 1, 2)
    n_v1 = ship(G_V1, V1, (0, 2), INNER, 4, 3, 3, 3)
    n_u2 = ship(G_U2, U2, (0, 2), AROUND, 2, 4, 4, 4)
    wait_group(G_GK, n_gk)
    chunk3 = min(8, ny)
    for a in range(0, ny, chunk3):
        k = GK[a:a + chunk3]
        up_y = [GK[j] if j < ny else blank for j in range(a + 1, a + chunk3 + 1)]
        down_y = [GK[j] if j >= 0 else blank for j in range(a - 1, a + chunk3 - 1)]
        y_next = 0.5 * (k + jnp.stack(up_y))
        y_previous = 0.5 * (k + jnp.stack(down_y))
        x_next = 0.5 * (k + jnp.where(at_x < nx - 1, next_x(k), 0.0))
        x_previous = 0.5 * (k + jnp.where(at_x > 0, previous_x(k), 0.0))
        z_next = 0.5 * (k + jnp.where(z < 31, roll(k, -1, 2), 0.0))
        z_previous = 0.5 * (k + jnp.where(z > 0, roll(k, 1, 2), 0.0))
        C3[0, a:a + chunk3] = y_previous
        C3[1, a:a + chunk3] = y_next
        C3[2, a:a + chunk3] = jnp.where(at_x < nx - 1, x_next, 0.0)
        C3[3, a:a + chunk3] = jnp.where((at_x > 0) & (at_x < nx), x_previous, 0.0)
        C3[4, a:a + chunk3] = jnp.where(z < 31, z_next, 0.0)
        C3[5, a:a + chunk3] = jnp.where(z > 0, z_previous, 0.0)
        C3[6, a:a + chunk3] = y_next + y_previous + x_next + x_previous + z_next + z_previous
    R3[0] = blank
    R3[ny + 1] = blank
    for a in range(0, ny, chunk3):
        P3[a:a + chunk3] = jnp.zeros((chunk3,) + shape, F32)
        Q3[a:a + chunk3] = jnp.zeros((chunk3,) + shape, F32)
        X3[2 + a:2 + a + chunk3] = jnp.zeros((chunk3,) + shape, F32)
    wait_group(G_GB, n_gb)
    for a in range(0, ny, chunk3):
        R3[1 + a:1 + a + chunk3] = GB[a:a + chunk3]

    def over_grid(x):
        x = jnp.sum(x, axis=0, keepdims=True)
        first = jnp.sum(jnp.where(first_rhs[0:1], x, 0.0), axis=1, keepdims=True)
        second = jnp.sum(jnp.where(first_rhs[0:1], 0.0, x), axis=1, keepdims=True)
        return jnp.where(first_rhs[0:1], first, second)

    def iteration(_, carry):
        norm_before, alpha_before = carry
        norm, energy = blank, blank
        for a in range(0, ny, chunk3):
            mid = R3[1 + a:1 + a + chunk3]
            beside = C3[0, a:a + chunk3] * R3[a:a + chunk3] + C3[1, a:a + chunk3] * R3[2 + a:2 + a + chunk3]
            beside += C3[2, a:a + chunk3] * next_x(mid) + C3[3, a:a + chunk3] * previous_x(mid)
            beside += C3[4, a:a + chunk3] * roll(mid, -1, 2) + C3[5, a:a + chunk3] * roll(mid, 1, 2)
            image = C3[6, a:a + chunk3] * mid - beside
            W3[a:a + chunk3] = image
            norm += jnp.sum(mid * mid, axis=0)
            energy += jnp.sum(mid * image, axis=0)
        norm, energy = over_grid(norm), over_grid(energy)
        beta = norm / norm_before
        alpha = norm / (energy - beta * norm / alpha_before)
        for a in range(0, ny, chunk3):
            p = R3[1 + a:1 + a + chunk3] + beta * P3[a:a + chunk3]
            q = W3[a:a + chunk3] + beta * Q3[a:a + chunk3]
            P3[a:a + chunk3] = p
            Q3[a:a + chunk3] = q
            X3[2 + a:2 + a + chunk3] += alpha * p
            R3[1 + a:1 + a + chunk3] -= alpha * q
        return norm, alpha

    lax.fori_loop(0, CSWEEPS, iteration, (jnp.full((1, 128), jnp.inf, F32), jnp.ones((1, 128), F32)))

    near = X3[pl.ds(gy, 5)]
    S5[:, 2:10, :] = near
    S5[:, 10:18, :] = roll(near, 64, 2)
    for dx in range(-2, 3):
        for dy in range(-2, 3):
            T5[dx + 2, pl.ds(dy % ROWS, 1), :] = S5[dy + 2, pl.ds(gx + (dx + 2), 1), :]

    lane2 = lane // 2
    row_low, row_high = sub // 2, 4 + sub // 2

    wait_group(G_U2, n_u2)
    for i in range(5):
        low = take_rows(take_lanes(T5[i, 0:8], lane2), row_low)
        high = take_rows(take_lanes(T5[i, 8:16], lane2), row_high)
        for p in (2 * i, 2 * i + 1):
            v = U2[1, p] + jnp.concatenate([low, high], axis=0)
            M2[p:p + 1] = jnp.where(inside((1, ROWS, 128), p - 4, 2, 4), v[None], 0.0)
    sweep(at(M2, 4), 4, at(U2, 4, 0), C2, 3, to(VA2, 3), -3, 8, 4)
    sweep(at(VA2, 3), 3, at(U2, 4, 0), C2, 3, to(VB2, 2), -2, 6, 6)

    wait_group(G_V1, n_v1)
    for p1 in range(-3, 7):
        e = VB2[p1 // 2 + 2]
        good = inside((1, ROWS, 128), p1, 4, 3)
        for k in range(2):
            index = lane2 + 64 * k
            low = take_rows(take_lanes(e[0:8], index), row_low)
            high = take_rows(take_lanes(e[8:16], index), row_high)
            v = V1[k, p1 + 3] + jnp.concatenate([low, high], axis=0)
            M1[k, p1 + 3:p1 + 4] = jnp.where(good, v[None], 0.0)
    for k in range(2):
        sweep(at(M1, 3, k), 3, b1[k], C1, 2, to(VA1, 2, k), -2, 8, 4)
    sweep(at(VA1, 2, 0), 2, b1[0], C1, 2, to(VB1, 1, 0), -1, 6, 6)

    def store_coarse(p, n, x):
        coarse_ref[pl.ds(p, n)] = x[:, 0:4]

    sweep(at(VA1, 2, 1), 2, b1[1], C1, 2, store_coarse, 0, 4, 4, 8)

    wait_group(G_V0, n_v0)
    for p1 in range(-1, 5):
        e = VB1[0, p1 + 1]
        pieces = []
        for k in range(2):
            index = lane2 + 64 * k
            first, second = take_lanes(e[0:8], index), take_lanes(e[8:16], index)
            low = take_rows(first, row_low)
            high = jnp.where(sub < 4, take_rows(first, row_high), take_rows(second, row_high))
            pieces.append(jnp.concatenate([low, high], axis=0))
        e = jnp.concatenate(pieces, axis=1)
        v = V0[2 * p1 + 2:2 * p1 + 4] + e[None]
        VA0[2 * p1 + 2:2 * p1 + 4] = jnp.where(inside(v.shape, 2 * p1, 8, 2), v, 0.0)
    sweep(at(VA0, 2), 2, at(S0, 2), C0, 2, to(VB0, 1), -1, 10, 2)
    sweep(at(VB0, 1), 1, at(S0, 2), C0, 2, to(fine_ref, 0), 0, 8, 2, 8)

    for group, rows in ((G_K0, n_k0), (G_S0, n_s0), (G_E1, n_e1), (G_K2, n_k2), (G_KC, n_kc), (G_KD, n_kd), (G_GK, n_gk), (G_B1, n_b1),
                        (G_BF, n_bf), (G_BC, n_bc), (G_GB, n_gb), (G_V0, n_v0), (G_V1, n_v1), (G_U2, n_u2)):
        wait_rows(rows, send_sem.at[group])


def put_out(fine, coarse, fine_out, coarse_out, sem):
    copies = [
        pltpu.make_async_copy(fine, fine_out, sem.at[0]),
        pltpu.make_async_copy(coarse, coarse_out, sem.at[1]),
    ]
    for copy in copies:
        copy.start()
    for copy in copies:
        copy.wait()


def solution(mesh):
    nx, ny = mesh.shape["gx"], mesh.shape["gy"]

    def vmem(*shape):
        return pltpu.VMEM(shape, F32)

    def on_device(source, kappa):
        scratch = [
            vmem(14, 16, 256), vmem(12, 16, 256), vmem(12, 16, 256), vmem(12, 16, 256), vmem(10, 16, 256),
            vmem(7, 13, 16, 256),
            vmem(2, 10, 16, 128), vmem(10, 16, 128), vmem(2, 10, 16, 128), vmem(2, 8, 16, 128), vmem(2, 6, 16, 128),
            vmem(7, 9, 16, 128), vmem(2, 10, 16, 128),
            vmem(10, 16, 128), vmem(2, 10, 16, 128), vmem(8, 16, 128), vmem(6, 16, 128),
            vmem(7, 9, 16, 128), vmem(10, 16, 128),
            vmem(nx, 8, 128), vmem(nx, 8, 128), vmem(nx, 8, 128),
            vmem(nx + 2, 8, 128), vmem(nx + 2, 8, 128), vmem(nx + 2, 8, 128),
            vmem(nx, 8, 128), vmem(nx, 8, 128), vmem(8, nx, 8, 128),
            vmem(16, 128), vmem(16, 128), vmem(ny, 8, 128), vmem(ny, 8, 128),
            vmem(7, ny, 8, 128), vmem(ny + 2, 8, 128), vmem(ny, 8, 128), vmem(ny, 8, 128), vmem(ny, 8, 128),
            vmem(ny + 4, 8, 128), vmem(5, 24, 128), vmem(5, 16, 128),
            vmem(512, 128),
            pltpu.SemaphoreType.DMA((2,)), pltpu.SemaphoreType.DMA((GROUPS,)), pltpu.SemaphoreType.DMA((GROUPS,)), pltpu.SemaphoreType.REGULAR((2,)),
        ]
        fine, coarse = pl.pallas_call(
            lambda *refs: kernel(nx, ny, *refs),
            out_shape=(jax.ShapeDtypeStruct((8, 8, 256), F32), jax.ShapeDtypeStruct((4, 4, 128), F32)),
            in_specs=[pl.BlockSpec(memory_space=pltpu.HBM)] * 2,
            out_specs=[pl.BlockSpec(memory_space=pltpu.VMEM)] * 2,
            scratch_shapes=scratch,
            compiler_params=pltpu.CompilerParams(
                collective_id=0, has_side_effects=True, vmem_limit_bytes=32 * 1024 * 1024
            ),
            name="vcycles",
        )(*(pltpu.with_memory_space_constraint(x, pltpu.HBM) for x in (source, kappa)))
        return pl.pallas_call(
            put_out,
            out_shape=(jax.ShapeDtypeStruct((8, 8, 256), F32), jax.ShapeDtypeStruct((4, 4, 128), F32)),
            in_specs=[pl.BlockSpec(memory_space=pltpu.VMEM)] * 2,
            out_specs=[pl.BlockSpec(memory_space=pltpu.HBM)] * 2,
            scratch_shapes=[pltpu.SemaphoreType.DMA((2,))],
            compiler_params=pltpu.CompilerParams(vmem_limit_bytes=4 * 1024 * 1024),
            name="put_out",
        )(fine, coarse)

    spec = P("gx", "gy", None)
    return jax.shard_map(on_device, mesh=mesh, in_specs=(spec, spec), out_specs=(spec, spec), check_vma=False)
```

```python
import jax
import jax.numpy as jnp
from jax import lax
from jax.experimental import pallas as pl
from jax.experimental.pallas import tpu as pltpu
from jax.sharding import PartitionSpec as P


CSWEEPS = 8
OMEGA = 0.8
REACH = 4
F32 = jnp.float32
ROWS = 16

INNER = [(-1, -1), (-1, 1), (1, -1), (1, 1), (-1, 0), (1, 0), (0, -1), (0, 1)]
AROUND = INNER + [
    (dx, dy) for dx in (-2, 2, -1, 1, 0) for dy in (-2, -1, 0, 1, 2) if max(abs(dx), abs(dy)) == 2
]

(G_K0, G_S0, G_E1, G_K2, G_KC, G_GK, G_B1, G_BF, G_BC, G_GB, G_V0, G_V1, G_U2, G_KD, G_BD) = range(15)
GROUPS = 15


def span(step, size, rim):
    low = max(0, step * size - rim)
    high = min(size, size + rim + step * size)
    return low, high - low, low - step * size


def roll(x, shift, axis):
    return pltpu.roll(x, shift % x.shape[axis], axis)


def iota(shape, axis):
    return lax.broadcasted_iota(jnp.int32, shape, axis)


def take_lanes(x, index):
    return jnp.take_along_axis(x, index, axis=1)


def take_rows(x, index):
    return jnp.take_along_axis(x, index, axis=0)


def pair_lanes(a, b):
    lane = iota(a.shape, 1)
    index = lax.rem(2 * lane, 128)
    a = take_lanes(a + roll(a, -1, 1), index)
    if b is None:
        return a
    b = take_lanes(b + roll(b, -1, 1), index)
    return jnp.where(lane < 64, a, b)


def pair_rows(x):
    return take_rows(x + roll(x, -1, 0), lax.rem(2 * iota(x.shape, 0), 8))


def kernel(nx, ny, src_hbm, kap_hbm, fine_ref, coarse_ref, K0, S0, V0, VA0, VB0, C0, E1, B1, V1, VA1, VB1, C1, M1,
           K2, U2, VA2, VB2, C2, M2, KC, BF, BC, KM, VC, WC, PF, PC, CC, ZK, ZB, GK, GB, C3, R3, W3, P3, Q3, X3, S5, T5, D, local_sem, send_sem, recv_sem, word):
    gx = lax.axis_index("gx")
    gy = lax.axis_index("gy")
    mesh_ids = pl.DeviceIdType.MESH

    def peer(dx, dy):
        return (lax.rem(gx + (dx + nx), nx) if not isinstance(dx, int) or dx else gx,
                lax.rem(gy + (dy + ny), ny) if not isinstance(dy, int) or dy else gy)

    def wait_rows(rows, sem):
        pltpu.make_async_copy(D.at[pl.ds(0, rows)], D.at[pl.ds(0, rows)], sem).wait()

    def wait_group(group, rows):
        wait_rows(rows, recv_sem.at[group])

    def ship(group, ref, lead, steps, size, rim, corner, offset):
        total = 0
        for dx, dy in steps:
            reach = corner if dx and dy else rim
            px, cx, qx = span(dx, size, reach)
            py, cy, qy = span(dy, size, reach)
            here = (pl.ds(px + offset, cx), pl.ds(py, cy), slice(None))
            there = (pl.ds(qx + offset, cx), pl.ds(qy % ROWS, cy), slice(None))
            if lead is not None:
                here, there = (pl.ds(*lead),) + here, (pl.ds(*lead),) + there
            pltpu.make_async_remote_copy(
                src_ref=ref.at[here], dst_ref=ref.at[there], send_sem=send_sem.at[group], recv_sem=recv_sem.at[group],
                device_id=peer(dx, dy), device_id_type=mesh_ids,
            ).start()
            total += cx * cy * (ref.shape[-1] // 128) * (lead[1] if lead else 1)
        return total

    pieces = {0: (0, 2, 0), -1: (0, 2, 2), 1: (0, 2, 6), -2: (0, 1, 4), 2: (1, 1, 5)}

    def ship_sides(group, ref, steps):
        total = 0
        for dy in steps:
            here, count, there = pieces[dy]
            pltpu.make_async_remote_copy(
                src_ref=ref.at[:, pl.ds(here, count), :], dst_ref=ref.at[:, pl.ds(there, count), :],
                send_sem=send_sem.at[group], recv_sem=recv_sem.at[group],
                device_id=peer(0, dy), device_id_type=mesh_ids,
            ).start()
            total += nx * count
        return total

    def ship_columns(group, ref, spread):
        def pass_on(x, steps):
            for dy in steps:
                here, count, there = pieces[dy]
                pltpu.make_async_remote_copy(
                    src_ref=ref.at[pl.ds(gx, 1), pl.ds(here, count), :], dst_ref=ref.at[pl.ds(gx, 1), pl.ds(there, count), :],
                    send_sem=send_sem.at[group], recv_sem=recv_sem.at[group],
                    device_id=(x, peer(0, dy)[1]), device_id_type=mesh_ids,
                ).start()

        sides = [dy for dy in (-2, 2, -1, 1) if abs(dy) <= spread]

        def step(i, carry):
            far = nx // 2 + (1 - 2 * lax.rem(i, 2)) * ((i + 1) // 2)
            pass_on(lax.rem(gx + far, nx), sides + [0])
            return carry

        lax.fori_loop(0, nx - 1, step, 0)
        pass_on(gx, sides)
        return 2 * (nx - 1) + nx * sum(pieces[dy][1] for dy in sides)

    def ship_row(group, ref):
        def step(i, carry):
            pltpu.make_async_remote_copy(
                src_ref=ref.at[gy], dst_ref=ref.at[gy], send_sem=send_sem.at[group],
                recv_sem=recv_sem.at[group], device_id=(gx, lax.rem(gy + i, ny)), device_id_type=mesh_ids,
            ).start()
            return carry
        lax.fori_loop(1, ny, step, 0)
        return 8 * (ny - 1)

    copies = [
        pltpu.make_async_copy(kap_hbm, K0.at[pl.ds(3, 8), pl.ds(0, 8), :], local_sem.at[0]),
        pltpu.make_async_copy(src_hbm, S0.at[pl.ds(2, 8), pl.ds(0, 8), :], local_sem.at[1]),
    ]
    for copy in copies:
        copy.start()
    barrier = pltpu.get_barrier_semaphore()

    def greet(device):
        pl.semaphore_signal(barrier, inc=1, device_id=device, device_id_type=mesh_ids)

    def greet_y(i, carry):
        greet((gx, lax.rem(gy + i, ny)))
        return carry

    near = range(1, nx) if nx <= 2 * REACH else [*range(1, REACH + 1), *range(nx - REACH, nx)]
    corners = [(dx, dy) for dx, dy in INNER if dx and dy]
    for dx in near:
        greet(peer(dx, 0))
    for dx, dy in corners:
        greet(peer(dx, dy))
    lax.fori_loop(1, ny, greet_y, 0)
    for copy in copies:
        copy.wait()

    def restrict0(ref, offset, scale):
        out = []
        for i in range(4):
            both = ref[offset + 2 * i, 0:8, :] + ref[offset + 2 * i + 1, 0:8, :]
            out.append(scale * pair_rows(pair_lanes(both[:, :128], both[:, 128:])))
        return out

    own1 = restrict0(K0, 3, 0.125)
    for i, tile in enumerate(own1):
        E1[1, 3 + i, 0:4, :] = tile[0:4]
    for i, tile in enumerate(restrict0(S0, 2, 0.5)):
        E1[0, 3 + i, 0:4, :] = tile[0:4]
    own2 = []
    for i in range(2):
        own2.append(0.125 * pair_rows(pair_lanes(own1[2 * i] + own1[2 * i + 1], None)))
        K2[4 + i, 0:2, :] = own2[i][0:2]
    KC[pl.ds(gx, 1), 0:2, :] = jnp.where(iota((8, 128), 1) < 64, own2[0], own2[1])[None, 0:2]

    pl.semaphore_wait(barrier, len(near) + ny - 1 + len(corners))
    n_k0 = ship(G_K0, K0, None, INNER, 8, 3, 2, 3)
    n_s0 = ship(G_S0, S0, None, INNER, 8, 2, 1, 2)
    if nx > 2 * REACH:
        for dx in (REACH, -REACH):
            pl.semaphore_signal(word.at[0], inc=1, device_id=peer(dx, 0), device_id_type=mesh_ids)
    n_e1 = ship(G_E1, E1, (0, 2), INNER, 4, 3, 3, 3)

    def inside(shape, first, size, rim):
        plane = iota(shape, 0) + first + gx * size
        row = iota(shape, 1)
        row = jnp.where(row < 8 + size // 2, row, row - ROWS)
        good = (row >= -rim) & (row < size + rim)
        row = row + gy * size
        return good & (plane >= 0) & (plane < nx * size) & (row >= 0) & (row < ny * size)

    def faces(read, C, planes, width, depth, size, rim, first, chunk):
        for a in range(0, planes, chunk):
            n = min(chunk, planes - a)
            k = read(a, n + 2)
            mid = k[1:n + 1]
            west = 0.5 * (k[0:n + 1] + k[1:n + 2])
            C[0, a:a + n + 1] = west
            north = 0.5 * (mid + roll(mid, -1, 1))
            south = roll(north, 1, 1)
            z = lax.rem(iota(mid.shape, 2), depth)
            top = z == depth - 1
            bottom = z == 0
            above = 0.5 * (mid + jnp.where(top, 0.0, roll(mid, -1, 2)))
            below = 0.5 * (mid + jnp.where(bottom, 0.0, roll(mid, 1, 2)))
            total = west[0:n] + west[1:n + 1] + north + south + above + below
            C[1, a:a + n] = north
            C[2, a:a + n] = south
            C[3, a:a + n] = jnp.where(top, 0.0, above)
            C[4, a:a + n] = jnp.where(bottom, 0.0, below)
            C[5, a:a + n] = total
            C[6, a:a + n] = jnp.where(inside(mid.shape, first + a, size, rim), OMEGA / total, 0.0)

    def residual(v, b, C, c, n, rows=ROWS):
        mid = v[1:n + 1]
        cut = slice(0, rows)
        beside = C[0, c:c + n, cut] * v[0:n, cut] + C[0, c + 1:c + n + 1, cut] * v[2:n + 2, cut]
        beside += C[1, c:c + n, cut] * roll(mid, -1, 1)[:, cut] + C[2, c:c + n, cut] * roll(mid, 1, 1)[:, cut]
        mid = mid[:, cut]
        beside += C[3, c:c + n, cut] * roll(mid, -1, 2) + C[4, c:c + n, cut] * roll(mid, 1, 2)
        return b - C[5, c:c + n, cut] * mid + beside

    def sweep(V, vo, b, C, co, store, first, planes, chunk, rows=ROWS):
        for a in range(0, planes, chunk):
            n = min(chunk, planes - a)
            p = first + a
            v = V(p - 1, n + 2)
            r = residual(v, b(p, n, rows), C, p + co, n, rows)
            store(p, n, v[1:n + 1, 0:rows] + C[6, p + co:p + co + n, 0:rows] * r)

    wait_group(G_K0, n_k0)
    n_k2 = ship(G_K2, K2, None, AROUND, 2, 4, 4, 4)
    if nx > 2 * REACH:
        pl.semaphore_wait(word.at[0], 2)
    for dy in (-1, 1):
        pl.semaphore_signal(word.at[1], inc=1, device_id=peer(0, dy), device_id_type=mesh_ids)

    def read_k0(a, n):
        k = K0[a:a + n]
        return jnp.where(inside(k.shape, a - 3, 8, 3), k, 0.0)

    faces(read_k0, C0, 12, 256, 256, 8, 3, -2, 2)
    wait_group(G_S0, n_s0)
    for a in range(0, 12, 2):
        VA0[a:a + 2] = C0[6, a:a + 2] * S0[a:a + 2]

    def at(ref, offset, lead=None):
        def read(p, n, rows=ROWS):
            where = (pl.ds(p + offset, n), pl.ds(0, rows), slice(None))
            return ref[where] if lead is None else ref[(lead,) + where]
        return read

    def to(ref, offset, lead=None):
        def store(p, n, x):
            where = (pl.ds(p + offset, n), pl.ds(0, x.shape[1]), slice(None))
            if lead is None:
                ref[where] = x
            else:
                ref[(lead,) + where] = x
        return store

    sweep(at(VA0, 2), 2, at(S0, 2), C0, 2, to(VB0, 1), -1, 10, 2)
    for i in range(4):
        r = residual(VB0[2 * i:2 * i + 4], S0[2 + 2 * i:4 + 2 * i, 0:8], C0, 2 + 2 * i, 2, 8)
        both = r[0] + r[1]
        B1[3 + i, 0:4, :] = 0.5 * pair_rows(pair_lanes(both[:, :128], both[:, 128:]))[0:4]
    n_b1 = ship(G_B1, B1, None, INNER, 4, 2, 2, 3)
    n_kc = ship_columns(G_KC, KC, 0)
    V0[2:10, 0:8, :] = VB0[1:9, 0:8, :]


    def packed(ref):
        keep = lax.rem(iota((8, 128), 0) + 8 * (iota((8, 128), 1) // 64), 16) < nx
        return jnp.where(keep, jnp.where(iota((8, 128), 1) < 64, ref[0:8], ref[8:16]), 0.0)

    wait_group(G_E1, n_e1)

    def read_k1(a, n):
        k = E1[1, a:a + n]
        return jnp.where(inside(k.shape, a - 3, 4, 3), k, 0.0)

    faces(read_k1, C1, 8, 128, 128, 4, 3, -2, 4)
    b1 = (at(B1, 3), at(E1, 3, 0))

    def down1(k):
        for a in range(0, 8, 4):
            VA1[k, a:a + 4] = C1[6, a:a + 4] * b1[k](a - 2, 4)
        sweep(at(VA1, 2, k), 2, b1[k], C1, 2, to(VB1, 1, k), -1, 6, 6)
        r = residual(VB1[k], b1[k](0, 4, 8), C1, 2, 4, 8)
        V1[k, 3:7, 0:4, :] = VB1[k, 1:5, 0:4, :]
        return r[0] + r[1], r[2] + r[3]

    lane = iota((8, 128), 1)
    sub = iota((8, 128), 0)

    def right2(pairs, ref):
        tiles = [0.5 * pair_rows(pair_lanes(x, None)) for x in pairs]
        ref[pl.ds(gx, 1), 0:2, :] = jnp.where(lane < 64, tiles[0], tiles[1])[None, 0:2]
        return tiles

    tiles_c = right2(down1(1), BC)
    n_bc = ship_columns(G_BC, BC, 0)
    wait_group(G_B1, n_b1)
    tiles_f = right2(down1(0), BF)
    pl.semaphore_wait(word.at[1], 2)
    n_bf = ship_columns(G_BF, BF, 1)
    for i in range(2):
        U2[0, 4 + i, 0:2, :] = jnp.where(lane < 64, tiles_f[i], tiles_c[i])[0:2]

    even = lane < 64
    deep = lax.rem(lane, 64)
    row = jnp.where(sub < 5, sub, sub - 8) + 2 * gy
    good2 = (row >= 0) & (row < 2 * ny)
    blank = jnp.zeros((8, 128), F32)
    chunk2 = min(8, nx)
    for ref in (KM, VC, WC):
        ref[0] = blank
        ref[nx + 1] = blank

    def beside_x(v):
        n = v.shape[0] - 2
        v = roll(v, 64, 2)
        return jnp.where(even, v[0:n], v[1:n + 1]), jnp.where(even, v[1:n + 1], v[2:n + 2])

    wait_group(G_KC, n_kc)
    n_kd = ship_sides(G_KD, KC, (-2, 2, -1, 1))
    wait_group(G_BC, n_bc)
    n_bd = ship_sides(G_BD, BC, (-1, 1))
    n_v0 = ship(G_V0, V0, None, INNER, 8, 2, 1, 2)
    n_v1 = ship(G_V1, V1, (0, 2), INNER, 4, 3, 3, 3)
    wait_group(G_K2, n_k2)

    def read_k2(a, n):
        k = K2[a:a + n]
        return jnp.where(inside(k.shape, a - 4, 2, 4), k, 0.0)

    faces(read_k2, C2, 8, 128, 64, 2, 4, -3, 4)
    wait_group(G_KD, n_kd)
    for i in range(nx):
        KM[1 + i] = jnp.where(good2, KC[i], 0.0)
    for a in range(0, nx, chunk2):
        k = KM[a:a + chunk2 + 2]
        mid = k[1:chunk2 + 1]
        previous, following = beside_x(k)
        west, east = 0.5 * (mid + previous), 0.5 * (mid + following)
        north = 0.5 * (mid + roll(mid, -1, 1))
        south = roll(north, 1, 1)
        above = 0.5 * (mid + jnp.where(deep == 63, 0.0, roll(mid, -1, 2)))
        below = 0.5 * (mid + jnp.where(deep == 0, 0.0, roll(mid, 1, 2)))
        total = west + east + north + south + above + below
        CC[0, a:a + chunk2] = west
        CC[1, a:a + chunk2] = east
        CC[2, a:a + chunk2] = north
        CC[3, a:a + chunk2] = south
        CC[4, a:a + chunk2] = jnp.where(deep == 63, 0.0, above)
        CC[5, a:a + chunk2] = jnp.where(deep == 0, 0.0, below)
        CC[6, a:a + chunk2] = total
        CC[7, a:a + chunk2] = jnp.where(good2, OMEGA / total, 0.0)

    def pooled(tile):
        tile = tile + roll(tile, 64, 1)
        return tile + roll(tile, -1, 0)

    for i in range(nx):
        ZK[i:i + 1, :] = 0.125 * pair_lanes(pooled(KM[1 + i]), None)[0:1]

    def packed(ref):
        keep = sub + 8 * (lane // 64) < nx
        return jnp.where(keep, jnp.where(lane < 64, ref[0:8], ref[8:16]), 0.0)

    GK[gy] = packed(ZK)
    n_gk = ship_row(G_GK, GK)

    def residual2(V, b, a, n):
        v = V[a:a + n + 2]
        mid = v[1:n + 1]
        previous, following = beside_x(v)
        c = [CC[j, a:a + n] for j in range(7)]
        beside = c[0] * previous + c[1] * following + c[2] * roll(mid, -1, 1) + c[3] * roll(mid, 1, 1)
        beside += c[4] * roll(mid, -1, 2) + c[5] * roll(mid, 1, 2)
        return b[a:a + n] - c[6] * mid + beside

    def down2(b, summed):
        for a in range(0, nx, chunk2):
            VC[1 + a:1 + a + chunk2] = CC[7, a:a + chunk2] * b[a:a + chunk2]
        for a in range(0, nx, chunk2):
            v = VC[1 + a:1 + a + chunk2] + CC[7, a:a + chunk2] * residual2(VC, b, a, chunk2)
            WC[1 + a:1 + a + chunk2] = v
        own = WC[pl.ds(1 + gx, 1)][0]
        for a in range(0, nx, chunk2):
            r = residual2(WC, b, a, chunk2)
            for i in range(chunk2):
                summed[a + i] = pooled(r[i])
        return own

    wait_group(G_BD, n_bd)
    own_c = down2(BC, PC)

    shape = (8, 128)
    half = lane // 64
    at_x = sub + 8 * half
    z = lax.rem(lane, 32)
    first_rhs = lax.rem(lane, 64) < 32

    def next_x(v):
        a = roll(v, -1, 1)
        return jnp.where(sub == 7, roll(a, 64, 2), a)

    def previous_x(v):
        a = roll(v, 1, 1)
        return jnp.where(sub == 0, roll(a, 64, 2), a)

    wait_group(G_BF, n_bf)
    own_f = down2(BF, PF)
    for i in range(nx):
        ZB[i:i + 1, :] = 0.5 * pair_lanes(jnp.where(even, PF[i], PC[i]), None)[0:1]
    GB[gy] = packed(ZB)
    n_gb = ship_row(G_GB, GB)
    U2[1, 4, 0:2, :] = jnp.where(even, own_f, roll(own_c, 64, 1))[0:2]
    U2[1, 5, 0:2, :] = jnp.where(even, roll(own_f, 64, 1), own_c)[0:2]
    n_u2 = ship(G_U2, U2, (0, 2), AROUND, 2, 4, 4, 4)
    wait_group(G_GK, n_gk)
    chunk3 = min(8, ny)
    for a in range(0, ny, chunk3):
        k = GK[a:a + chunk3]
        up_y = [GK[j] if j < ny else blank for j in range(a + 1, a + chunk3 + 1)]
        down_y = [GK[j] if j >= 0 else blank for j in range(a - 1, a + chunk3 - 1)]
        y_next = 0.5 * (k + jnp.stack(up_y))
        y_previous = 0.5 * (k + jnp.stack(down_y))
        x_next = 0.5 * (k + jnp.where(at_x < nx - 1, next_x(k), 0.0))
        x_previous = 0.5 * (k + jnp.where(at_x > 0, previous_x(k), 0.0))
        z_next = 0.5 * (k + jnp.where(z < 31, roll(k, -1, 2), 0.0))
        z_previous = 0.5 * (k + jnp.where(z > 0, roll(k, 1, 2), 0.0))
        C3[0, a:a + chunk3] = y_previous
        C3[1, a:a + chunk3] = y_next
        C3[2, a:a + chunk3] = jnp.where(at_x < nx - 1, x_next, 0.0)
        C3[3, a:a + chunk3] = jnp.where((at_x > 0) & (at_x < nx), x_previous, 0.0)
        C3[4, a:a + chunk3] = jnp.where(z < 31, z_next, 0.0)
        C3[5, a:a + chunk3] = jnp.where(z > 0, z_previous, 0.0)
        C3[6, a:a + chunk3] = y_next + y_previous + x_next + x_previous + z_next + z_previous
    R3[0] = blank
    R3[ny + 1] = blank
    for a in range(0, ny, chunk3):
        P3[a:a + chunk3] = jnp.zeros((chunk3,) + shape, F32)
        Q3[a:a + chunk3] = jnp.zeros((chunk3,) + shape, F32)
        X3[2 + a:2 + a + chunk3] = jnp.zeros((chunk3,) + shape, F32)
    wait_group(G_GB, n_gb)
    for a in range(0, ny, chunk3):
        R3[1 + a:1 + a + chunk3] = GB[a:a + chunk3]

    def over_grid(x):
        x = jnp.sum(x, axis=0, keepdims=True)
        first = jnp.sum(jnp.where(first_rhs[0:1], x, 0.0), axis=1, keepdims=True)
        second = jnp.sum(jnp.where(first_rhs[0:1], 0.0, x), axis=1, keepdims=True)
        return jnp.where(first_rhs[0:1], first, second)

    def iteration(_, carry):
        norm_before, alpha_before = carry
        norm, energy = blank, blank
        for a in range(0, ny, chunk3):
            mid = R3[1 + a:1 + a + chunk3]
            beside = C3[0, a:a + chunk3] * R3[a:a + chunk3] + C3[1, a:a + chunk3] * R3[2 + a:2 + a + chunk3]
            beside += C3[2, a:a + chunk3] * next_x(mid) + C3[3, a:a + chunk3] * previous_x(mid)
            beside += C3[4, a:a + chunk3] * roll(mid, -1, 2) + C3[5, a:a + chunk3] * roll(mid, 1, 2)
            image = C3[6, a:a + chunk3] * mid - beside
            W3[a:a + chunk3] = image
            norm += jnp.sum(mid * mid, axis=0)
            energy += jnp.sum(mid * image, axis=0)
        norm, energy = over_grid(norm), over_grid(energy)
        beta = norm / norm_before
        alpha = norm / (energy - beta * norm / alpha_before)
        for a in range(0, ny, chunk3):
            p = R3[1 + a:1 + a + chunk3] + beta * P3[a:a + chunk3]
            q = W3[a:a + chunk3] + beta * Q3[a:a + chunk3]
            P3[a:a + chunk3] = p
            Q3[a:a + chunk3] = q
            X3[2 + a:2 + a + chunk3] += alpha * p
            R3[1 + a:1 + a + chunk3] -= alpha * q
        return norm, alpha

    lax.fori_loop(0, CSWEEPS, iteration, (jnp.full((1, 128), jnp.inf, F32), jnp.ones((1, 128), F32)))

    near = X3[pl.ds(gy, 5)]
    S5[:, 2:10, :] = near
    S5[:, 10:18, :] = roll(near, 64, 2)
    for dx in range(-2, 3):
        for dy in range(-2, 3):
            T5[dx + 2, pl.ds(dy % ROWS, 1), :] = S5[dy + 2, pl.ds(gx + (dx + 2), 1), :]

    lane2 = lane // 2
    row_low, row_high = sub // 2, 4 + sub // 2

    wait_group(G_U2, n_u2)
    for i in range(5):
        low = take_rows(take_lanes(T5[i, 0:8], lane2), row_low)
        high = take_rows(take_lanes(T5[i, 8:16], lane2), row_high)
        for p in (2 * i, 2 * i + 1):
            v = U2[1, p] + jnp.concatenate([low, high], axis=0)
            M2[p:p + 1] = jnp.where(inside((1, ROWS, 128), p - 4, 2, 4), v[None], 0.0)
    sweep(at(M2, 4), 4, at(U2, 4, 0), C2, 3, to(VA2, 3), -3, 8, 4)
    sweep(at(VA2, 3), 3, at(U2, 4, 0), C2, 3, to(VB2, 2), -2, 6, 6)

    wait_group(G_V1, n_v1)
    for p1 in range(-3, 7):
        e = VB2[p1 // 2 + 2]
        good = inside((1, ROWS, 128), p1, 4, 3)
        for k in range(2):
            index = lane2 + 64 * k
            low = take_rows(take_lanes(e[0:8], index), row_low)
            high = take_rows(take_lanes(e[8:16], index), row_high)
            v = V1[k, p1 + 3] + jnp.concatenate([low, high], axis=0)
            M1[k, p1 + 3:p1 + 4] = jnp.where(good, v[None], 0.0)
    for k in range(2):
        sweep(at(M1, 3, k), 3, b1[k], C1, 2, to(VA1, 2, k), -2, 8, 4)
    sweep(at(VA1, 2, 0), 2, b1[0], C1, 2, to(VB1, 1, 0), -1, 6, 6)

    def store_coarse(p, n, x):
        coarse_ref[pl.ds(p, n)] = x[:, 0:4]

    sweep(at(VA1, 2, 1), 2, b1[1], C1, 2, store_coarse, 0, 4, 4, 8)

    wait_group(G_V0, n_v0)
    for p1 in range(-1, 5):
        e = VB1[0, p1 + 1]
        pieces = []
        for k in range(2):
            index = lane2 + 64 * k
            first, second = take_lanes(e[0:8], index), take_lanes(e[8:16], index)
            low = take_rows(first, row_low)
            high = jnp.where(sub < 4, take_rows(first, row_high), take_rows(second, row_high))
            pieces.append(jnp.concatenate([low, high], axis=0))
        e = jnp.concatenate(pieces, axis=1)
        v = V0[2 * p1 + 2:2 * p1 + 4] + e[None]
        VA0[2 * p1 + 2:2 * p1 + 4] = jnp.where(inside(v.shape, 2 * p1, 8, 2), v, 0.0)
    sweep(at(VA0, 2), 2, at(S0, 2), C0, 2, to(VB0, 1), -1, 10, 2)
    sweep(at(VB0, 1), 1, at(S0, 2), C0, 2, to(fine_ref, 0), 0, 8, 2, 8)

    for group, rows in ((G_K0, n_k0), (G_S0, n_s0), (G_E1, n_e1), (G_K2, n_k2), (G_KC, n_kc), (G_KD, n_kd), (G_BD, n_bd), (G_GK, n_gk), (G_B1, n_b1),
                        (G_BF, n_bf), (G_BC, n_bc), (G_GB, n_gb), (G_V0, n_v0), (G_V1, n_v1), (G_U2, n_u2)):
        wait_rows(rows, send_sem.at[group])


def put_out(fine, coarse, fine_out, coarse_out, sem):
    copies = [
        pltpu.make_async_copy(fine, fine_out, sem.at[0]),
        pltpu.make_async_copy(coarse, coarse_out, sem.at[1]),
    ]
    for copy in copies:
        copy.start()
    for copy in copies:
        copy.wait()


def solution(mesh):
    nx, ny = mesh.shape["gx"], mesh.shape["gy"]

    def vmem(*shape):
        return pltpu.VMEM(shape, F32)

    def on_device(source, kappa):
        scratch = [
            vmem(14, 16, 256), vmem(12, 16, 256), vmem(12, 16, 256), vmem(12, 16, 256), vmem(10, 16, 256),
            vmem(7, 13, 16, 256),
            vmem(2, 10, 16, 128), vmem(10, 16, 128), vmem(2, 10, 16, 128), vmem(2, 8, 16, 128), vmem(2, 6, 16, 128),
            vmem(7, 9, 16, 128), vmem(2, 10, 16, 128),
            vmem(10, 16, 128), vmem(2, 10, 16, 128), vmem(8, 16, 128), vmem(6, 16, 128),
            vmem(7, 9, 16, 128), vmem(10, 16, 128),
            vmem(nx, 8, 128), vmem(nx, 8, 128), vmem(nx, 8, 128),
            vmem(nx + 2, 8, 128), vmem(nx + 2, 8, 128), vmem(nx + 2, 8, 128),
            vmem(nx, 8, 128), vmem(nx, 8, 128), vmem(8, nx, 8, 128),
            vmem(16, 128), vmem(16, 128), vmem(ny, 8, 128), vmem(ny, 8, 128),
            vmem(7, ny, 8, 128), vmem(ny + 2, 8, 128), vmem(ny, 8, 128), vmem(ny, 8, 128), vmem(ny, 8, 128),
            vmem(ny + 4, 8, 128), vmem(5, 24, 128), vmem(5, 16, 128),
            vmem(512, 128),
            pltpu.SemaphoreType.DMA((2,)), pltpu.SemaphoreType.DMA((GROUPS,)), pltpu.SemaphoreType.DMA((GROUPS,)), pltpu.SemaphoreType.REGULAR((2,)),
        ]
        fine, coarse = pl.pallas_call(
            lambda *refs: kernel(nx, ny, *refs),
            out_shape=(jax.ShapeDtypeStruct((8, 8, 256), F32), jax.ShapeDtypeStruct((4, 4, 128), F32)),
            in_specs=[pl.BlockSpec(memory_space=pltpu.HBM)] * 2,
            out_specs=[pl.BlockSpec(memory_space=pltpu.VMEM)] * 2,
            scratch_shapes=scratch,
            compiler_params=pltpu.CompilerParams(
                collective_id=0, has_side_effects=True, vmem_limit_bytes=32 * 1024 * 1024
            ),
            name="vcycles",
        )(*(pltpu.with_memory_space_constraint(x, pltpu.HBM) for x in (source, kappa)))
        return pl.pallas_call(
            put_out,
            out_shape=(jax.ShapeDtypeStruct((8, 8, 256), F32), jax.ShapeDtypeStruct((4, 4, 128), F32)),
            in_specs=[pl.BlockSpec(memory_space=pltpu.VMEM)] * 2,
            out_specs=[pl.BlockSpec(memory_space=pltpu.HBM)] * 2,
            scratch_shapes=[pltpu.SemaphoreType.DMA((2,))],
            compiler_params=pltpu.CompilerParams(vmem_limit_bytes=4 * 1024 * 1024),
            name="put_out",
        )(fine, coarse)

    spec = P("gx", "gy", None)
    return jax.shard_map(on_device, mesh=mesh, in_specs=(spec, spec), out_specs=(spec, spec), check_vma=False)
```

```python
import jax
import jax.numpy as jnp
from jax import lax
from jax.experimental import pallas as pl
from jax.experimental.pallas import tpu as pltpu
from jax.sharding import PartitionSpec as P


CSWEEPS = 8
OMEGA = 0.8
REACH = 4
F32 = jnp.float32
ROWS = 16

INNER = [(-1, -1), (-1, 1), (1, -1), (1, 1), (-1, 0), (1, 0), (0, -1), (0, 1)]
AROUND = INNER + [
    (dx, dy) for dx in (-2, 2, -1, 1, 0) for dy in (-2, -1, 0, 1, 2) if max(abs(dx), abs(dy)) == 2
]

(G_K0, G_S0, G_E1, G_K2, G_KC, G_GK, G_B1, G_BF, G_BC, G_GB, G_V0, G_V1, G_U2, G_KD, G_BD) = range(15)
GROUPS = 15


def span(step, size, rim):
    low = max(0, step * size - rim)
    high = min(size, size + rim + step * size)
    return low, high - low, low - step * size


def roll(x, shift, axis):
    return pltpu.roll(x, shift % x.shape[axis], axis)


def iota(shape, axis):
    return lax.broadcasted_iota(jnp.int32, shape, axis)


def take_lanes(x, index):
    return jnp.take_along_axis(x, index, axis=1)


def take_rows(x, index):
    return jnp.take_along_axis(x, index, axis=0)


def pair_lanes(a, b):
    lane = iota(a.shape, 1)
    index = lax.rem(2 * lane, 128)
    a = take_lanes(a + roll(a, -1, 1), index)
    if b is None:
        return a
    b = take_lanes(b + roll(b, -1, 1), index)
    return jnp.where(lane < 64, a, b)


def pair_rows(x):
    return take_rows(x + roll(x, -1, 0), lax.rem(2 * iota(x.shape, 0), 8))


def kernel(nx, ny, src_hbm, kap_hbm, fine_ref, coarse_ref, K0, S0, V0, VA0, VB0, C0, E1, B1, V1, VA1, VB1, C1, M1,
           K2, U2, VA2, VB2, C2, M2, KC, BF, BC, KM, VC, WC, PF, PC, CC, ZK, ZB, GK, GB, C3, R3, W3, P3, Q3, X3, S5, T5, D, local_sem, send_sem, recv_sem, word):
    gx = lax.axis_index("gx")
    gy = lax.axis_index("gy")
    mesh_ids = pl.DeviceIdType.MESH

    def peer(dx, dy):
        return (lax.rem(gx + (dx + nx), nx) if not isinstance(dx, int) or dx else gx,
                lax.rem(gy + (dy + ny), ny) if not isinstance(dy, int) or dy else gy)

    def wait_rows(rows, sem):
        pltpu.make_async_copy(D.at[pl.ds(0, rows)], D.at[pl.ds(0, rows)], sem).wait()

    def wait_group(group, rows):
        wait_rows(rows, recv_sem.at[group])

    def ship(group, ref, lead, steps, size, rim, corner, offset):
        total = 0
        for dx, dy in steps:
            reach = corner if dx and dy else rim
            px, cx, qx = span(dx, size, reach)
            py, cy, qy = span(dy, size, reach)
            here = (pl.ds(px + offset, cx), pl.ds(py, cy), slice(None))
            there = (pl.ds(qx + offset, cx), pl.ds(qy % ROWS, cy), slice(None))
            if lead is not None:
                here, there = (pl.ds(*lead),) + here, (pl.ds(*lead),) + there
            pltpu.make_async_remote_copy(
                src_ref=ref.at[here], dst_ref=ref.at[there], send_sem=send_sem.at[group], recv_sem=recv_sem.at[group],
                device_id=peer(dx, dy), device_id_type=mesh_ids,
            ).start()
            total += cx * cy * (ref.shape[-1] // 128) * (lead[1] if lead else 1)
        return total

    pieces = {0: (0, 2, 0), -1: (0, 2, 2), 1: (0, 2, 6), -2: (0, 1, 4), 2: (1, 1, 5)}

    def ship_sides(group, ref, steps):
        total = 0
        for dy in steps:
            here, count, there = pieces[dy]
            pltpu.make_async_remote_copy(
                src_ref=ref.at[:, pl.ds(here, count), :], dst_ref=ref.at[:, pl.ds(there, count), :],
                send_sem=send_sem.at[group], recv_sem=recv_sem.at[group],
                device_id=peer(0, dy), device_id_type=mesh_ids,
            ).start()
            total += nx * count
        return total

    def ship_columns(group, ref, spread):
        def pass_on(x, steps):
            for dy in steps:
                here, count, there = pieces[dy]
                pltpu.make_async_remote_copy(
                    src_ref=ref.at[pl.ds(gx, 1), pl.ds(here, count), :], dst_ref=ref.at[pl.ds(gx, 1), pl.ds(there, count), :],
                    send_sem=send_sem.at[group], recv_sem=recv_sem.at[group],
                    device_id=(x, peer(0, dy)[1]), device_id_type=mesh_ids,
                ).start()

        sides = [dy for dy in (-2, 2, -1, 1) if abs(dy) <= spread]

        def step(i, carry):
            far = nx // 2 + (1 - 2 * lax.rem(i, 2)) * ((i + 1) // 2)
            pass_on(lax.rem(gx + far, nx), sides + [0])
            return carry

        lax.fori_loop(0, nx - 1, step, 0)
        pass_on(gx, sides)
        return 2 * (nx - 1) + nx * sum(pieces[dy][1] for dy in sides)

    def ship_row(group, ref):
        def step(i, carry):
            pltpu.make_async_remote_copy(
                src_ref=ref.at[gy], dst_ref=ref.at[gy], send_sem=send_sem.at[group],
                recv_sem=recv_sem.at[group], device_id=(gx, lax.rem(gy + i, ny)), device_id_type=mesh_ids,
            ).start()
            return carry
        lax.fori_loop(1, ny, step, 0)
        return 8 * (ny - 1)

    copies = [
        pltpu.make_async_copy(kap_hbm, K0.at[pl.ds(3, 8), pl.ds(0, 8), :], local_sem.at[0]),
        pltpu.make_async_copy(src_hbm, S0.at[pl.ds(2, 8), pl.ds(0, 8), :], local_sem.at[1]),
    ]
    for copy in copies:
        copy.start()
    barrier = pltpu.get_barrier_semaphore()

    def greet(device):
        pl.semaphore_signal(barrier, inc=1, device_id=device, device_id_type=mesh_ids)

    near = range(1, nx) if nx <= 2 * REACH else [*range(1, REACH + 1), *range(nx - REACH, nx)]
    near_row = range(1, ny) if ny <= 4 else [1, 2, ny - 2, ny - 1]
    corners = [(dx, dy) for dx, dy in INNER if dx and dy]
    strides = [2 ** k for k in range(1, 8) if 2 ** k < ny // 2]

    def tell_row(k):
        if k < len(strides):
            for dy in (strides[k], -strides[k]):
                pl.semaphore_signal(word.at[2 + k], inc=1, device_id=peer(0, dy), device_id_type=mesh_ids)

    def hear_row(k):
        if k < len(strides):
            pl.semaphore_wait(word.at[2 + k], 2)

    for dx, dy in corners:
        greet(peer(dx, dy))
    for dx in near:
        greet(peer(dx, 0))
    for dy in near_row:
        greet(peer(0, dy))
    for copy in copies:
        copy.wait()

    def restrict0(ref, offset, scale):
        out = []
        for i in range(4):
            both = ref[offset + 2 * i, 0:8, :] + ref[offset + 2 * i + 1, 0:8, :]
            out.append(scale * pair_rows(pair_lanes(both[:, :128], both[:, 128:])))
        return out

    own1 = restrict0(K0, 3, 0.125)
    for i, tile in enumerate(own1):
        E1[1, 3 + i, 0:4, :] = tile[0:4]
    for i, tile in enumerate(restrict0(S0, 2, 0.5)):
        E1[0, 3 + i, 0:4, :] = tile[0:4]
    own2 = []
    for i in range(2):
        own2.append(0.125 * pair_rows(pair_lanes(own1[2 * i] + own1[2 * i + 1], None)))
        K2[4 + i, 0:2, :] = own2[i][0:2]
    KC[pl.ds(gx, 1), 0:2, :] = jnp.where(iota((8, 128), 1) < 64, own2[0], own2[1])[None, 0:2]

    pl.semaphore_wait(barrier, len(near) + len(near_row) + len(corners))
    tell_row(0)
    n_k0 = ship(G_K0, K0, None, INNER, 8, 3, 2, 3)
    n_s0 = ship(G_S0, S0, None, INNER, 8, 2, 1, 2)
    if nx > 2 * REACH:
        for dx in (REACH, -REACH):
            pl.semaphore_signal(word.at[0], inc=1, device_id=peer(dx, 0), device_id_type=mesh_ids)
    n_e1 = ship(G_E1, E1, (0, 2), INNER, 4, 3, 3, 3)

    def inside(shape, first, size, rim):
        plane = iota(shape, 0) + first + gx * size
        row = iota(shape, 1)
        row = jnp.where(row < 8 + size // 2, row, row - ROWS)
        good = (row >= -rim) & (row < size + rim)
        row = row + gy * size
        return good & (plane >= 0) & (plane < nx * size) & (row >= 0) & (row < ny * size)

    def faces(read, C, planes, width, depth, size, rim, first, chunk):
        for a in range(0, planes, chunk):
            n = min(chunk, planes - a)
            k = read(a, n + 2)
            mid = k[1:n + 1]
            west = 0.5 * (k[0:n + 1] + k[1:n + 2])
            C[0, a:a + n + 1] = west
            north = 0.5 * (mid + roll(mid, -1, 1))
            south = roll(north, 1, 1)
            z = lax.rem(iota(mid.shape, 2), depth)
            top = z == depth - 1
            bottom = z == 0
            above = 0.5 * (mid + jnp.where(top, 0.0, roll(mid, -1, 2)))
            below = 0.5 * (mid + jnp.where(bottom, 0.0, roll(mid, 1, 2)))
            total = west[0:n] + west[1:n + 1] + north + south + above + below
            C[1, a:a + n] = north
            C[2, a:a + n] = south
            C[3, a:a + n] = jnp.where(top, 0.0, above)
            C[4, a:a + n] = jnp.where(bottom, 0.0, below)
            C[5, a:a + n] = total
            C[6, a:a + n] = jnp.where(inside(mid.shape, first + a, size, rim), OMEGA / total, 0.0)

    def residual(v, b, C, c, n, rows=ROWS):
        mid = v[1:n + 1]
        cut = slice(0, rows)
        beside = C[0, c:c + n, cut] * v[0:n, cut] + C[0, c + 1:c + n + 1, cut] * v[2:n + 2, cut]
        beside += C[1, c:c + n, cut] * roll(mid, -1, 1)[:, cut] + C[2, c:c + n, cut] * roll(mid, 1, 1)[:, cut]
        mid = mid[:, cut]
        beside += C[3, c:c + n, cut] * roll(mid, -1, 2) + C[4, c:c + n, cut] * roll(mid, 1, 2)
        return b - C[5, c:c + n, cut] * mid + beside

    def sweep(V, vo, b, C, co, store, first, planes, chunk, rows=ROWS):
        for a in range(0, planes, chunk):
            n = min(chunk, planes - a)
            p = first + a
            v = V(p - 1, n + 2)
            r = residual(v, b(p, n, rows), C, p + co, n, rows)
            store(p, n, v[1:n + 1, 0:rows] + C[6, p + co:p + co + n, 0:rows] * r)

    wait_group(G_K0, n_k0)
    n_k2 = ship(G_K2, K2, None, AROUND, 2, 4, 4, 4)
    hear_row(0)
    tell_row(1)
    if nx > 2 * REACH:
        pl.semaphore_wait(word.at[0], 2)
    for dy in (-1, 1):
        pl.semaphore_signal(word.at[1], inc=1, device_id=peer(0, dy), device_id_type=mesh_ids)

    def read_k0(a, n):
        k = K0[a:a + n]
        return jnp.where(inside(k.shape, a - 3, 8, 3), k, 0.0)

    faces(read_k0, C0, 12, 256, 256, 8, 3, -2, 2)
    wait_group(G_S0, n_s0)
    for a in range(0, 12, 2):
        VA0[a:a + 2] = C0[6, a:a + 2] * S0[a:a + 2]

    def at(ref, offset, lead=None):
        def read(p, n, rows=ROWS):
            where = (pl.ds(p + offset, n), pl.ds(0, rows), slice(None))
            return ref[where] if lead is None else ref[(lead,) + where]
        return read

    def to(ref, offset, lead=None):
        def store(p, n, x):
            where = (pl.ds(p + offset, n), pl.ds(0, x.shape[1]), slice(None))
            if lead is None:
                ref[where] = x
            else:
                ref[(lead,) + where] = x
        return store

    sweep(at(VA0, 2), 2, at(S0, 2), C0, 2, to(VB0, 1), -1, 10, 2)
    for i in range(4):
        r = residual(VB0[2 * i:2 * i + 4], S0[2 + 2 * i:4 + 2 * i, 0:8], C0, 2 + 2 * i, 2, 8)
        both = r[0] + r[1]
        B1[3 + i, 0:4, :] = 0.5 * pair_rows(pair_lanes(both[:, :128], both[:, 128:]))[0:4]
    n_b1 = ship(G_B1, B1, None, INNER, 4, 2, 2, 3)
    n_kc = ship_columns(G_KC, KC, 0)
    V0[2:10, 0:8, :] = VB0[1:9, 0:8, :]


    def packed(ref):
        keep = lax.rem(iota((8, 128), 0) + 8 * (iota((8, 128), 1) // 64), 16) < nx
        return jnp.where(keep, jnp.where(iota((8, 128), 1) < 64, ref[0:8], ref[8:16]), 0.0)

    wait_group(G_E1, n_e1)

    def read_k1(a, n):
        k = E1[1, a:a + n]
        return jnp.where(inside(k.shape, a - 3, 4, 3), k, 0.0)

    faces(read_k1, C1, 8, 128, 128, 4, 3, -2, 4)
    b1 = (at(B1, 3), at(E1, 3, 0))

    def down1(k):
        for a in range(0, 8, 4):
            VA1[k, a:a + 4] = C1[6, a:a + 4] * b1[k](a - 2, 4)
        sweep(at(VA1, 2, k), 2, b1[k], C1, 2, to(VB1, 1, k), -1, 6, 6)
        r = residual(VB1[k], b1[k](0, 4, 8), C1, 2, 4, 8)
        V1[k, 3:7, 0:4, :] = VB1[k, 1:5, 0:4, :]
        return r[0] + r[1], r[2] + r[3]

    lane = iota((8, 128), 1)
    sub = iota((8, 128), 0)

    def right2(pairs, ref):
        tiles = [0.5 * pair_rows(pair_lanes(x, None)) for x in pairs]
        ref[pl.ds(gx, 1), 0:2, :] = jnp.where(lane < 64, tiles[0], tiles[1])[None, 0:2]
        return tiles

    tiles_c = right2(down1(1), BC)
    n_bc = ship_columns(G_BC, BC, 0)
    wait_group(G_B1, n_b1)
    tiles_f = right2(down1(0), BF)
    pl.semaphore_wait(word.at[1], 2)
    n_bf = ship_columns(G_BF, BF, 1)
    hear_row(1)
    tell_row(2)
    for i in range(2):
        U2[0, 4 + i, 0:2, :] = jnp.where(lane < 64, tiles_f[i], tiles_c[i])[0:2]

    even = lane < 64
    deep = lax.rem(lane, 64)
    row = jnp.where(sub < 5, sub, sub - 8) + 2 * gy
    good2 = (row >= 0) & (row < 2 * ny)
    blank = jnp.zeros((8, 128), F32)
    chunk2 = min(8, nx)
    for ref in (KM, VC, WC):
        ref[0] = blank
        ref[nx + 1] = blank

    def beside_x(v):
        n = v.shape[0] - 2
        v = roll(v, 64, 2)
        return jnp.where(even, v[0:n], v[1:n + 1]), jnp.where(even, v[1:n + 1], v[2:n + 2])

    wait_group(G_KC, n_kc)
    n_kd = ship_sides(G_KD, KC, (-2, 2, -1, 1))
    wait_group(G_BC, n_bc)
    n_bd = ship_sides(G_BD, BC, (-1, 1))
    n_v0 = ship(G_V0, V0, None, INNER, 8, 2, 1, 2)
    n_v1 = ship(G_V1, V1, (0, 2), INNER, 4, 3, 3, 3)
    wait_group(G_K2, n_k2)

    def read_k2(a, n):
        k = K2[a:a + n]
        return jnp.where(inside(k.shape, a - 4, 2, 4), k, 0.0)

    faces(read_k2, C2, 8, 128, 64, 2, 4, -3, 4)
    wait_group(G_KD, n_kd)
    for i in range(nx):
        KM[1 + i] = jnp.where(good2, KC[i], 0.0)
    for a in range(0, nx, chunk2):
        k = KM[a:a + chunk2 + 2]
        mid = k[1:chunk2 + 1]
        previous, following = beside_x(k)
        west, east = 0.5 * (mid + previous), 0.5 * (mid + following)
        north = 0.5 * (mid + roll(mid, -1, 1))
        south = roll(north, 1, 1)
        above = 0.5 * (mid + jnp.where(deep == 63, 0.0, roll(mid, -1, 2)))
        below = 0.5 * (mid + jnp.where(deep == 0, 0.0, roll(mid, 1, 2)))
        total = west + east + north + south + above + below
        CC[0, a:a + chunk2] = west
        CC[1, a:a + chunk2] = east
        CC[2, a:a + chunk2] = north
        CC[3, a:a + chunk2] = south
        CC[4, a:a + chunk2] = jnp.where(deep == 63, 0.0, above)
        CC[5, a:a + chunk2] = jnp.where(deep == 0, 0.0, below)
        CC[6, a:a + chunk2] = total
        CC[7, a:a + chunk2] = jnp.where(good2, OMEGA / total, 0.0)

    def pooled(tile):
        tile = tile + roll(tile, 64, 1)
        return tile + roll(tile, -1, 0)

    for i in range(nx):
        ZK[i:i + 1, :] = 0.125 * pair_lanes(pooled(KM[1 + i]), None)[0:1]

    def packed(ref):
        keep = sub + 8 * (lane // 64) < nx
        return jnp.where(keep, jnp.where(lane < 64, ref[0:8], ref[8:16]), 0.0)

    for k in range(2, len(strides)):
        hear_row(k)
        tell_row(k + 1)
    GK[gy] = packed(ZK)
    n_gk = ship_row(G_GK, GK)

    def residual2(V, b, a, n):
        v = V[a:a + n + 2]
        mid = v[1:n + 1]
        previous, following = beside_x(v)
        c = [CC[j, a:a + n] for j in range(7)]
        beside = c[0] * previous + c[1] * following + c[2] * roll(mid, -1, 1) + c[3] * roll(mid, 1, 1)
        beside += c[4] * roll(mid, -1, 2) + c[5] * roll(mid, 1, 2)
        return b[a:a + n] - c[6] * mid + beside

    def down2(b, summed):
        for a in range(0, nx, chunk2):
            VC[1 + a:1 + a + chunk2] = CC[7, a:a + chunk2] * b[a:a + chunk2]
        for a in range(0, nx, chunk2):
            v = VC[1 + a:1 + a + chunk2] + CC[7, a:a + chunk2] * residual2(VC, b, a, chunk2)
            WC[1 + a:1 + a + chunk2] = v
        own = WC[pl.ds(1 + gx, 1)][0]
        for a in range(0, nx, chunk2):
            r = residual2(WC, b, a, chunk2)
            for i in range(chunk2):
                summed[a + i] = pooled(r[i])
        return own

    wait_group(G_BD, n_bd)
    own_c = down2(BC, PC)

    shape = (8, 128)
    half = lane // 64
    at_x = sub + 8 * half
    z = lax.rem(lane, 32)
    first_rhs = lax.rem(lane, 64) < 32

    def next_x(v):
        a = roll(v, -1, 1)
        return jnp.where(sub == 7, roll(a, 64, 2), a)

    def previous_x(v):
        a = roll(v, 1, 1)
        return jnp.where(sub == 0, roll(a, 64, 2), a)

    wait_group(G_BF, n_bf)
    own_f = down2(BF, PF)
    for i in range(nx):
        ZB[i:i + 1, :] = 0.5 * pair_lanes(jnp.where(even, PF[i], PC[i]), None)[0:1]
    GB[gy] = packed(ZB)
    n_gb = ship_row(G_GB, GB)
    U2[1, 4, 0:2, :] = jnp.where(even, own_f, roll(own_c, 64, 1))[0:2]
    U2[1, 5, 0:2, :] = jnp.where(even, roll(own_f, 64, 1), own_c)[0:2]
    n_u2 = ship(G_U2, U2, (0, 2), AROUND, 2, 4, 4, 4)
    wait_group(G_GK, n_gk)
    chunk3 = min(8, ny)
    for a in range(0, ny, chunk3):
        k = GK[a:a + chunk3]
        up_y = [GK[j] if j < ny else blank for j in range(a + 1, a + chunk3 + 1)]
        down_y = [GK[j] if j >= 0 else blank for j in range(a - 1, a + chunk3 - 1)]
        y_next = 0.5 * (k + jnp.stack(up_y))
        y_previous = 0.5 * (k + jnp.stack(down_y))
        x_next = 0.5 * (k + jnp.where(at_x < nx - 1, next_x(k), 0.0))
        x_previous = 0.5 * (k + jnp.where(at_x > 0, previous_x(k), 0.0))
        z_next = 0.5 * (k + jnp.where(z < 31, roll(k, -1, 2), 0.0))
        z_previous = 0.5 * (k + jnp.where(z > 0, roll(k, 1, 2), 0.0))
        C3[0, a:a + chunk3] = y_previous
        C3[1, a:a + chunk3] = y_next
        C3[2, a:a + chunk3] = jnp.where(at_x < nx - 1, x_next, 0.0)
        C3[3, a:a + chunk3] = jnp.where((at_x > 0) & (at_x < nx), x_previous, 0.0)
        C3[4, a:a + chunk3] = jnp.where(z < 31, z_next, 0.0)
        C3[5, a:a + chunk3] = jnp.where(z > 0, z_previous, 0.0)
        C3[6, a:a + chunk3] = y_next + y_previous + x_next + x_previous + z_next + z_previous
    R3[0] = blank
    R3[ny + 1] = blank
    for a in range(0, ny, chunk3):
        P3[a:a + chunk3] = jnp.zeros((chunk3,) + shape, F32)
        Q3[a:a + chunk3] = jnp.zeros((chunk3,) + shape, F32)
        X3[2 + a:2 + a + chunk3] = jnp.zeros((chunk3,) + shape, F32)
    wait_group(G_GB, n_gb)
    for a in range(0, ny, chunk3):
        R3[1 + a:1 + a + chunk3] = GB[a:a + chunk3]

    def over_grid(x):
        x = jnp.sum(x, axis=0, keepdims=True)
        first = jnp.sum(jnp.where(first_rhs[0:1], x, 0.0), axis=1, keepdims=True)
        second = jnp.sum(jnp.where(first_rhs[0:1], 0.0, x), axis=1, keepdims=True)
        return jnp.where(first_rhs[0:1], first, second)

    def iteration(_, carry):
        norm_before, alpha_before = carry
        norm, energy = blank, blank
        for a in range(0, ny, chunk3):
            mid = R3[1 + a:1 + a + chunk3]
            beside = C3[0, a:a + chunk3] * R3[a:a + chunk3] + C3[1, a:a + chunk3] * R3[2 + a:2 + a + chunk3]
            beside += C3[2, a:a + chunk3] * next_x(mid) + C3[3, a:a + chunk3] * previous_x(mid)
            beside += C3[4, a:a + chunk3] * roll(mid, -1, 2) + C3[5, a:a + chunk3] * roll(mid, 1, 2)
            image = C3[6, a:a + chunk3] * mid - beside
            W3[a:a + chunk3] = image
            norm += jnp.sum(mid * mid, axis=0)
            energy += jnp.sum(mid * image, axis=0)
        norm, energy = over_grid(norm), over_grid(energy)
        beta = norm / norm_before
        alpha = norm / (energy - beta * norm / alpha_before)
        for a in range(0, ny, chunk3):
            p = R3[1 + a:1 + a + chunk3] + beta * P3[a:a + chunk3]
            q = W3[a:a + chunk3] + beta * Q3[a:a + chunk3]
            P3[a:a + chunk3] = p
            Q3[a:a + chunk3] = q
            X3[2 + a:2 + a + chunk3] += alpha * p
            R3[1 + a:1 + a + chunk3] -= alpha * q
        return norm, alpha

    lax.fori_loop(0, CSWEEPS, iteration, (jnp.full((1, 128), jnp.inf, F32), jnp.ones((1, 128), F32)))

    near = X3[pl.ds(gy, 5)]
    S5[:, 2:10, :] = near
    S5[:, 10:18, :] = roll(near, 64, 2)
    for dx in range(-2, 3):
        for dy in range(-2, 3):
            T5[dx + 2, pl.ds(dy % ROWS, 1), :] = S5[dy + 2, pl.ds(gx + (dx + 2), 1), :]

    lane2 = lane // 2
    row_low, row_high = sub // 2, 4 + sub // 2

    wait_group(G_U2, n_u2)
    for i in range(5):
        low = take_rows(take_lanes(T5[i, 0:8], lane2), row_low)
        high = take_rows(take_lanes(T5[i, 8:16], lane2), row_high)
        for p in (2 * i, 2 * i + 1):
            v = U2[1, p] + jnp.concatenate([low, high], axis=0)
            M2[p:p + 1] = jnp.where(inside((1, ROWS, 128), p - 4, 2, 4), v[None], 0.0)
    sweep(at(M2, 4), 4, at(U2, 4, 0), C2, 3, to(VA2, 3), -3, 8, 4)
    sweep(at(VA2, 3), 3, at(U2, 4, 0), C2, 3, to(VB2, 2), -2, 6, 6)

    wait_group(G_V1, n_v1)
    for p1 in range(-3, 7):
        e = VB2[p1 // 2 + 2]
        good = inside((1, ROWS, 128), p1, 4, 3)
        for k in range(2):
            index = lane2 + 64 * k
            low = take_rows(take_lanes(e[0:8], index), row_low)
            high = take_rows(take_lanes(e[8:16], index), row_high)
            v = V1[k, p1 + 3] + jnp.concatenate([low, high], axis=0)
            M1[k, p1 + 3:p1 + 4] = jnp.where(good, v[None], 0.0)
    for k in range(2):
        sweep(at(M1, 3, k), 3, b1[k], C1, 2, to(VA1, 2, k), -2, 8, 4)
    sweep(at(VA1, 2, 0), 2, b1[0], C1, 2, to(VB1, 1, 0), -1, 6, 6)

    def store_coarse(p, n, x):
        coarse_ref[pl.ds(p, n)] = x[:, 0:4]

    sweep(at(VA1, 2, 1), 2, b1[1], C1, 2, store_coarse, 0, 4, 4, 8)

    wait_group(G_V0, n_v0)
    for p1 in range(-1, 5):
        e = VB1[0, p1 + 1]
        pieces = []
        for k in range(2):
            index = lane2 + 64 * k
            first, second = take_lanes(e[0:8], index), take_lanes(e[8:16], index)
            low = take_rows(first, row_low)
            high = jnp.where(sub < 4, take_rows(first, row_high), take_rows(second, row_high))
            pieces.append(jnp.concatenate([low, high], axis=0))
        e = jnp.concatenate(pieces, axis=1)
        v = V0[2 * p1 + 2:2 * p1 + 4] + e[None]
        VA0[2 * p1 + 2:2 * p1 + 4] = jnp.where(inside(v.shape, 2 * p1, 8, 2), v, 0.0)
    sweep(at(VA0, 2), 2, at(S0, 2), C0, 2, to(VB0, 1), -1, 10, 2)
    sweep(at(VB0, 1), 1, at(S0, 2), C0, 2, to(fine_ref, 0), 0, 8, 2, 8)

    for group, rows in ((G_K0, n_k0), (G_S0, n_s0), (G_E1, n_e1), (G_K2, n_k2), (G_KC, n_kc), (G_KD, n_kd), (G_BD, n_bd), (G_GK, n_gk), (G_B1, n_b1),
                        (G_BF, n_bf), (G_BC, n_bc), (G_GB, n_gb), (G_V0, n_v0), (G_V1, n_v1), (G_U2, n_u2)):
        wait_rows(rows, send_sem.at[group])


def put_out(fine, coarse, fine_out, coarse_out, sem):
    copies = [
        pltpu.make_async_copy(fine, fine_out, sem.at[0]),
        pltpu.make_async_copy(coarse, coarse_out, sem.at[1]),
    ]
    for copy in copies:
        copy.start()
    for copy in copies:
        copy.wait()


def solution(mesh):
    nx, ny = mesh.shape["gx"], mesh.shape["gy"]

    def vmem(*shape):
        return pltpu.VMEM(shape, F32)

    def on_device(source, kappa):
        scratch = [
            vmem(14, 16, 256), vmem(12, 16, 256), vmem(12, 16, 256), vmem(12, 16, 256), vmem(10, 16, 256),
            vmem(7, 13, 16, 256),
            vmem(2, 10, 16, 128), vmem(10, 16, 128), vmem(2, 10, 16, 128), vmem(2, 8, 16, 128), vmem(2, 6, 16, 128),
            vmem(7, 9, 16, 128), vmem(2, 10, 16, 128),
            vmem(10, 16, 128), vmem(2, 10, 16, 128), vmem(8, 16, 128), vmem(6, 16, 128),
            vmem(7, 9, 16, 128), vmem(10, 16, 128),
            vmem(nx, 8, 128), vmem(nx, 8, 128), vmem(nx, 8, 128),
            vmem(nx + 2, 8, 128), vmem(nx + 2, 8, 128), vmem(nx + 2, 8, 128),
            vmem(nx, 8, 128), vmem(nx, 8, 128), vmem(8, nx, 8, 128),
            vmem(16, 128), vmem(16, 128), vmem(ny, 8, 128), vmem(ny, 8, 128),
            vmem(7, ny, 8, 128), vmem(ny + 2, 8, 128), vmem(ny, 8, 128), vmem(ny, 8, 128), vmem(ny, 8, 128),
            vmem(ny + 4, 8, 128), vmem(5, 24, 128), vmem(5, 16, 128),
            vmem(512, 128),
            pltpu.SemaphoreType.DMA((2,)), pltpu.SemaphoreType.DMA((GROUPS,)), pltpu.SemaphoreType.DMA((GROUPS,)), pltpu.SemaphoreType.REGULAR((10,)),
        ]
        fine, coarse = pl.pallas_call(
            lambda *refs: kernel(nx, ny, *refs),
            out_shape=(jax.ShapeDtypeStruct((8, 8, 256), F32), jax.ShapeDtypeStruct((4, 4, 128), F32)),
            in_specs=[pl.BlockSpec(memory_space=pltpu.HBM)] * 2,
            out_specs=[pl.BlockSpec(memory_space=pltpu.VMEM)] * 2,
            scratch_shapes=scratch,
            compiler_params=pltpu.CompilerParams(
                collective_id=0, has_side_effects=True, vmem_limit_bytes=32 * 1024 * 1024
            ),
            name="vcycles",
        )(*(pltpu.with_memory_space_constraint(x, pltpu.HBM) for x in (source, kappa)))
        return pl.pallas_call(
            put_out,
            out_shape=(jax.ShapeDtypeStruct((8, 8, 256), F32), jax.ShapeDtypeStruct((4, 4, 128), F32)),
            in_specs=[pl.BlockSpec(memory_space=pltpu.VMEM)] * 2,
            out_specs=[pl.BlockSpec(memory_space=pltpu.HBM)] * 2,
            scratch_shapes=[pltpu.SemaphoreType.DMA((2,))],
            compiler_params=pltpu.CompilerParams(vmem_limit_bytes=4 * 1024 * 1024),
            name="put_out",
        )(fine, coarse)

    spec = P("gx", "gy", None)
    return jax.shard_map(on_device, mesh=mesh, in_specs=(spec, spec), out_specs=(spec, spec), check_vma=False)
```

```python
import jax
import jax.numpy as jnp
from jax import lax
from jax.experimental import pallas as pl
from jax.experimental.pallas import tpu as pltpu
from jax.sharding import PartitionSpec as P


CSWEEPS = 8
OMEGA = 0.8
REACH = 4
F32 = jnp.float32
ROWS = 16

INNER = [(-1, -1), (-1, 1), (1, -1), (1, 1), (-1, 0), (1, 0), (0, -1), (0, 1)]
AROUND = INNER + [
    (dx, dy) for dx in (-2, 2, -1, 1, 0) for dy in (-2, -1, 0, 1, 2) if max(abs(dx), abs(dy)) == 2
]

(G_K0, G_S0, G_E1, G_K2, G_KC, G_GK, G_B1, G_BF, G_BC, G_GB, G_V0, G_V1, G_U2, G_KD, G_BD) = range(15)
GROUPS = 15


def span(step, size, rim):
    low = max(0, step * size - rim)
    high = min(size, size + rim + step * size)
    return low, high - low, low - step * size


def roll(x, shift, axis):
    return pltpu.roll(x, shift % x.shape[axis], axis)


def iota(shape, axis):
    return lax.broadcasted_iota(jnp.int32, shape, axis)


def take_lanes(x, index):
    return jnp.take_along_axis(x, index, axis=1)


def take_rows(x, index):
    return jnp.take_along_axis(x, index, axis=0)


def pair_lanes(a, b):
    lane = iota(a.shape, 1)
    index = lax.rem(2 * lane, 128)
    a = take_lanes(a + roll(a, -1, 1), index)
    if b is None:
        return a
    b = take_lanes(b + roll(b, -1, 1), index)
    return jnp.where(lane < 64, a, b)


def pair_rows(x):
    return take_rows(x + roll(x, -1, 0), lax.rem(2 * iota(x.shape, 0), 8))


def kernel(nx, ny, src_hbm, kap_hbm, fine_ref, coarse_ref, K0, S0, V0, VA0, VB0, C0, E1, B1, V1, VA1, VB1, C1, M1,
           K2, U2, VA2, VB2, C2, M2, KC, BF, BC, KM, VC, WC, PF, PC, CC, ZK, ZB, GK, GB, C3, R3, W3, P3, Q3, X3, S5, T5, D, local_sem, send_sem, recv_sem, word):
    gx = lax.axis_index("gx")
    gy = lax.axis_index("gy")
    mesh_ids = pl.DeviceIdType.MESH

    def peer(dx, dy):
        return (lax.rem(gx + (dx + nx), nx) if not isinstance(dx, int) or dx else gx,
                lax.rem(gy + (dy + ny), ny) if not isinstance(dy, int) or dy else gy)

    def wait_rows(rows, sem):
        pltpu.make_async_copy(D.at[pl.ds(0, rows)], D.at[pl.ds(0, rows)], sem).wait()

    def wait_group(group, rows):
        wait_rows(rows, recv_sem.at[group])

    def ship(group, ref, lead, steps, size, rim, corner, offset):
        total = 0
        for dx, dy in steps:
            reach = corner if dx and dy else rim
            px, cx, qx = span(dx, size, reach[0])
            py, cy, qy = span(dy, size, reach[1])
            here = (pl.ds(px + offset, cx), pl.ds(py, cy), slice(None))
            there = (pl.ds(qx + offset, cx), pl.ds(qy % ROWS, cy), slice(None))
            if lead is not None:
                here, there = (pl.ds(*lead),) + here, (pl.ds(*lead),) + there
            pltpu.make_async_remote_copy(
                src_ref=ref.at[here], dst_ref=ref.at[there], send_sem=send_sem.at[group], recv_sem=recv_sem.at[group],
                device_id=peer(dx, dy), device_id_type=mesh_ids,
            ).start()
            total += cx * cy * (ref.shape[-1] // 128) * (lead[1] if lead else 1)
        return total

    pieces = {0: (0, 2, 0), -1: (0, 2, 2), 1: (0, 2, 6), -2: (0, 1, 4), 2: (1, 1, 5)}

    def ship_sides(group, ref, steps):
        total = 0
        for dy in steps:
            here, count, there = pieces[dy]
            pltpu.make_async_remote_copy(
                src_ref=ref.at[:, pl.ds(here, count), :], dst_ref=ref.at[:, pl.ds(there, count), :],
                send_sem=send_sem.at[group], recv_sem=recv_sem.at[group],
                device_id=peer(0, dy), device_id_type=mesh_ids,
            ).start()
            total += nx * count
        return total

    def ship_columns(group, ref, spread):
        def pass_on(x, steps):
            for dy in steps:
                here, count, there = pieces[dy]
                pltpu.make_async_remote_copy(
                    src_ref=ref.at[pl.ds(gx, 1), pl.ds(here, count), :], dst_ref=ref.at[pl.ds(gx, 1), pl.ds(there, count), :],
                    send_sem=send_sem.at[group], recv_sem=recv_sem.at[group],
                    device_id=(x, peer(0, dy)[1]), device_id_type=mesh_ids,
                ).start()

        sides = [dy for dy in (-2, 2, -1, 1) if abs(dy) <= spread]

        def step(i, carry):
            far = nx // 2 + (1 - 2 * lax.rem(i, 2)) * ((i + 1) // 2)
            pass_on(lax.rem(gx + far, nx), sides + [0])
            return carry

        lax.fori_loop(0, nx - 1, step, 0)
        pass_on(gx, sides)
        return 2 * (nx - 1) + nx * sum(pieces[dy][1] for dy in sides)

    def ship_row(group, ref):
        def step(i, carry):
            pltpu.make_async_remote_copy(
                src_ref=ref.at[gy], dst_ref=ref.at[gy], send_sem=send_sem.at[group],
                recv_sem=recv_sem.at[group], device_id=(gx, lax.rem(gy + i, ny)), device_id_type=mesh_ids,
            ).start()
            return carry
        lax.fori_loop(1, ny, step, 0)
        return 8 * (ny - 1)

    copies = [
        pltpu.make_async_copy(kap_hbm, K0.at[pl.ds(5, 8), pl.ds(0, 8), :], local_sem.at[0]),
        pltpu.make_async_copy(src_hbm, S0.at[pl.ds(4, 8), pl.ds(0, 8), :], local_sem.at[1]),
    ]
    for copy in copies:
        copy.start()
    barrier = pltpu.get_barrier_semaphore()

    def greet(device):
        pl.semaphore_signal(barrier, inc=1, device_id=device, device_id_type=mesh_ids)

    near = range(1, nx) if nx <= 2 * REACH else [*range(1, REACH + 1), *range(nx - REACH, nx)]
    near_row = range(1, ny) if ny <= 4 else [1, 2, ny - 2, ny - 1]
    corners = [(dx, dy) for dx, dy in INNER if dx and dy]
    strides = [2 ** k for k in range(1, 8) if 2 ** k < ny // 2]

    def tell_row(k):
        if k < len(strides):
            for dy in (strides[k], -strides[k]):
                pl.semaphore_signal(word.at[2 + k], inc=1, device_id=peer(0, dy), device_id_type=mesh_ids)

    def hear_row(k):
        if k < len(strides):
            pl.semaphore_wait(word.at[2 + k], 2)

    for dx, dy in corners:
        greet(peer(dx, dy))
    for dx in near:
        greet(peer(dx, 0))
    for dy in near_row:
        greet(peer(0, dy))
    for copy in copies:
        copy.wait()

    def restrict0(ref, offset, scale):
        out = []
        for i in range(4):
            both = ref[offset + 2 * i, 0:8, :] + ref[offset + 2 * i + 1, 0:8, :]
            out.append(scale * pair_rows(pair_lanes(both[:, :128], both[:, 128:])))
        return out

    own1 = restrict0(K0, 5, 0.125)
    for i, tile in enumerate(own1):
        E1[1, 3 + i, 0:4, :] = tile[0:4]
    for i, tile in enumerate(restrict0(S0, 4, 0.5)):
        E1[0, 3 + i, 0:4, :] = tile[0:4]
    own2 = []
    for i in range(2):
        own2.append(0.125 * pair_rows(pair_lanes(own1[2 * i] + own1[2 * i + 1], None)))
        K2[4 + i, 0:2, :] = own2[i][0:2]
    KC[pl.ds(gx, 1), 0:2, :] = jnp.where(iota((8, 128), 1) < 64, own2[0], own2[1])[None, 0:2]

    pl.semaphore_wait(barrier, len(near) + len(near_row) + len(corners))
    tell_row(0)
    n_k0 = ship(G_K0, K0, None, INNER, 8, (5, 3), (4, 3), 5)
    n_s0 = ship(G_S0, S0, None, INNER, 8, (4, 2), (3, 2), 4)
    if nx > 2 * REACH:
        for dx in (REACH, -REACH):
            pl.semaphore_signal(word.at[0], inc=1, device_id=peer(dx, 0), device_id_type=mesh_ids)
    n_e1 = ship(G_E1, E1, (0, 2), INNER, 4, (3, 3), (3, 3), 3)

    def inside(shape, first, size, rim):
        plane = iota(shape, 0) + first + gx * size
        row = iota(shape, 1)
        row = jnp.where(row < 8 + size // 2, row, row - ROWS)
        good = (row >= -rim) & (row < size + rim)
        row = row + gy * size
        return good & (plane >= 0) & (plane < nx * size) & (row >= 0) & (row < ny * size)

    def faces(read, C, planes, width, depth, size, rim, first, chunk):
        for a in range(0, planes, chunk):
            n = min(chunk, planes - a)
            k = read(a, n + 2)
            mid = k[1:n + 1]
            west = 0.5 * (k[0:n + 1] + k[1:n + 2])
            C[0, a:a + n + 1] = west
            north = 0.5 * (mid + roll(mid, -1, 1))
            south = roll(north, 1, 1)
            z = lax.rem(iota(mid.shape, 2), depth)
            top = z == depth - 1
            bottom = z == 0
            above = 0.5 * (mid + jnp.where(top, 0.0, roll(mid, -1, 2)))
            below = 0.5 * (mid + jnp.where(bottom, 0.0, roll(mid, 1, 2)))
            total = west[0:n] + west[1:n + 1] + north + south + above + below
            C[1, a:a + n] = north
            C[2, a:a + n] = south
            C[3, a:a + n] = jnp.where(top, 0.0, above)
            C[4, a:a + n] = jnp.where(bottom, 0.0, below)
            C[5, a:a + n] = total
            C[6, a:a + n] = jnp.where(inside(mid.shape, first + a, size, rim), OMEGA / total, 0.0)

    def residual(v, b, C, c, n, rows=ROWS):
        mid = v[1:n + 1]
        cut = slice(0, rows)
        beside = C[0, c:c + n, cut] * v[0:n, cut] + C[0, c + 1:c + n + 1, cut] * v[2:n + 2, cut]
        beside += C[1, c:c + n, cut] * roll(mid, -1, 1)[:, cut] + C[2, c:c + n, cut] * roll(mid, 1, 1)[:, cut]
        mid = mid[:, cut]
        beside += C[3, c:c + n, cut] * roll(mid, -1, 2) + C[4, c:c + n, cut] * roll(mid, 1, 2)
        return b - C[5, c:c + n, cut] * mid + beside

    def sweep(V, vo, b, C, co, store, first, planes, chunk, rows=ROWS):
        for a in range(0, planes, chunk):
            n = min(chunk, planes - a)
            p = first + a
            v = V(p - 1, n + 2)
            r = residual(v, b(p, n, rows), C, p + co, n, rows)
            store(p, n, v[1:n + 1, 0:rows] + C[6, p + co:p + co + n, 0:rows] * r)

    wait_group(G_K0, n_k0)
    n_k2 = ship(G_K2, K2, None, AROUND, 2, (4, 4), (4, 4), 4)
    hear_row(0)
    tell_row(1)
    if nx > 2 * REACH:
        pl.semaphore_wait(word.at[0], 2)
    for dy in (-1, 1):
        pl.semaphore_signal(word.at[1], inc=1, device_id=peer(0, dy), device_id_type=mesh_ids)

    def read_k0(a, n):
        k = K0[a:a + n]
        return jnp.where(inside(k.shape, a - 5, 8, 3), k, 0.0)

    faces(read_k0, C0, 16, 256, 256, 8, 3, -4, 2)
    wait_group(G_S0, n_s0)
    for a in range(0, 16, 2):
        VA0[a:a + 2] = C0[6, a:a + 2] * S0[a:a + 2]

    def at(ref, offset, lead=None):
        def read(p, n, rows=ROWS):
            where = (pl.ds(p + offset, n), pl.ds(0, rows), slice(None))
            return ref[where] if lead is None else ref[(lead,) + where]
        return read

    def to(ref, offset, lead=None):
        def store(p, n, x):
            where = (pl.ds(p + offset, n), pl.ds(0, x.shape[1]), slice(None))
            if lead is None:
                ref[where] = x
            else:
                ref[(lead,) + where] = x
        return store

    sweep(at(VA0, 4), 4, at(S0, 4), C0, 4, to(VB0, 3), -3, 14, 2)
    for i in range(6):
        r = residual(VB0[2 * i:2 * i + 4], S0[2 + 2 * i:4 + 2 * i, 0:8], C0, 2 + 2 * i, 2, 8)
        both = r[0] + r[1]
        cells = 0.5 * pair_rows(pair_lanes(both[:, :128], both[:, 128:]))[0:4]
        B1[2 + i, 0:4, :] = cells
        if 1 <= i <= 4:
            V1[2, 2 + i, 0:4, :] = cells
    n_b1 = 0
    for dx, dy, planes, rows, land, row in (
        (0, 1, (2, 6), (2, 2), 2, 14), (0, -1, (2, 6), (0, 2), 2, 4), (1, 0, (5, 1), (0, 4), 1, 0), (-1, 0, (4, 1), (0, 4), 8, 0)
    ):
        pltpu.make_async_remote_copy(
            src_ref=B1.at[pl.ds(*planes), pl.ds(*rows), :], dst_ref=B1.at[pl.ds(land, planes[1]), pl.ds(row, rows[1]), :],
            send_sem=send_sem.at[G_B1], recv_sem=recv_sem.at[G_B1], device_id=peer(dx, dy), device_id_type=mesh_ids,
        ).start()
        n_b1 += planes[1] * rows[1]
    n_kc = ship_columns(G_KC, KC, 0)
    V0[2:10, 0:8, :] = VB0[3:11, 0:8, :]


    def packed(ref):
        keep = lax.rem(iota((8, 128), 0) + 8 * (iota((8, 128), 1) // 64), 16) < nx
        return jnp.where(keep, jnp.where(iota((8, 128), 1) < 64, ref[0:8], ref[8:16]), 0.0)

    wait_group(G_E1, n_e1)

    def read_k1(a, n):
        k = E1[1, a:a + n]
        return jnp.where(inside(k.shape, a - 3, 4, 3), k, 0.0)

    faces(read_k1, C1, 8, 128, 128, 4, 3, -2, 4)
    b1 = (at(B1, 3), at(E1, 3, 0))

    def down1(k):
        for a in range(0, 8, 4):
            VA1[k, a:a + 4] = C1[6, a:a + 4] * b1[k](a - 2, 4)
        sweep(at(VA1, 2, k), 2, b1[k], C1, 2, to(VB1, 1, k), -1, 6, 6)
        r = residual(VB1[k], b1[k](0, 4, 8), C1, 2, 4, 8)
        V1[k, 3:7, 0:4, :] = VB1[k, 1:5, 0:4, :]
        return r[0] + r[1], r[2] + r[3]

    lane = iota((8, 128), 1)
    sub = iota((8, 128), 0)

    def right2(pairs, ref):
        tiles = [0.5 * pair_rows(pair_lanes(x, None)) for x in pairs]
        ref[pl.ds(gx, 1), 0:2, :] = jnp.where(lane < 64, tiles[0], tiles[1])[None, 0:2]
        return tiles

    tiles_c = right2(down1(1), BC)
    n_bc = ship_columns(G_BC, BC, 0)
    wait_group(G_B1, n_b1)
    tiles_f = right2(down1(0), BF)
    pl.semaphore_wait(word.at[1], 2)
    n_bf = ship_columns(G_BF, BF, 1)
    hear_row(1)
    tell_row(2)
    for i in range(2):
        U2[0, 4 + i, 0:2, :] = jnp.where(lane < 64, tiles_f[i], tiles_c[i])[0:2]

    even = lane < 64
    deep = lax.rem(lane, 64)
    row = jnp.where(sub < 5, sub, sub - 8) + 2 * gy
    good2 = (row >= 0) & (row < 2 * ny)
    blank = jnp.zeros((8, 128), F32)
    chunk2 = min(8, nx)
    for ref in (KM, VC, WC):
        ref[0] = blank
        ref[nx + 1] = blank

    def beside_x(v):
        n = v.shape[0] - 2
        v = roll(v, 64, 2)
        return jnp.where(even, v[0:n], v[1:n + 1]), jnp.where(even, v[1:n + 1], v[2:n + 2])

    wait_group(G_KC, n_kc)
    n_kd = ship_sides(G_KD, KC, (-2, 2, -1, 1))
    wait_group(G_BC, n_bc)
    n_bd = ship_sides(G_BD, BC, (-1, 1))
    n_v0 = ship(G_V0, V0, None, INNER, 8, (2, 2), (1, 1), 2)
    n_v1 = ship(G_V1, V1, (0, 3), INNER, 4, (3, 3), (3, 3), 3)
    wait_group(G_K2, n_k2)

    def read_k2(a, n):
        k = K2[a:a + n]
        return jnp.where(inside(k.shape, a - 4, 2, 4), k, 0.0)

    faces(read_k2, C2, 8, 128, 64, 2, 4, -3, 4)
    wait_group(G_KD, n_kd)
    for i in range(nx):
        KM[1 + i] = jnp.where(good2, KC[i], 0.0)
    for a in range(0, nx, chunk2):
        k = KM[a:a + chunk2 + 2]
        mid = k[1:chunk2 + 1]
        previous, following = beside_x(k)
        west, east = 0.5 * (mid + previous), 0.5 * (mid + following)
        north = 0.5 * (mid + roll(mid, -1, 1))
        south = roll(north, 1, 1)
        above = 0.5 * (mid + jnp.where(deep == 63, 0.0, roll(mid, -1, 2)))
        below = 0.5 * (mid + jnp.where(deep == 0, 0.0, roll(mid, 1, 2)))
        total = west + east + north + south + above + below
        CC[0, a:a + chunk2] = west
        CC[1, a:a + chunk2] = east
        CC[2, a:a + chunk2] = north
        CC[3, a:a + chunk2] = south
        CC[4, a:a + chunk2] = jnp.where(deep == 63, 0.0, above)
        CC[5, a:a + chunk2] = jnp.where(deep == 0, 0.0, below)
        CC[6, a:a + chunk2] = total
        CC[7, a:a + chunk2] = jnp.where(good2, OMEGA / total, 0.0)

    def pooled(tile):
        tile = tile + roll(tile, 64, 1)
        return tile + roll(tile, -1, 0)

    for i in range(nx):
        ZK[i:i + 1, :] = 0.125 * pair_lanes(pooled(KM[1 + i]), None)[0:1]

    def packed(ref):
        keep = sub + 8 * (lane // 64) < nx
        return jnp.where(keep, jnp.where(lane < 64, ref[0:8], ref[8:16]), 0.0)

    for k in range(2, len(strides)):
        hear_row(k)
        tell_row(k + 1)
    GK[gy] = packed(ZK)
    n_gk = ship_row(G_GK, GK)

    def residual2(V, b, a, n):
        v = V[a:a + n + 2]
        mid = v[1:n + 1]
        previous, following = beside_x(v)
        c = [CC[j, a:a + n] for j in range(7)]
        beside = c[0] * previous + c[1] * following + c[2] * roll(mid, -1, 1) + c[3] * roll(mid, 1, 1)
        beside += c[4] * roll(mid, -1, 2) + c[5] * roll(mid, 1, 2)
        return b[a:a + n] - c[6] * mid + beside

    def down2(b, summed):
        for a in range(0, nx, chunk2):
            VC[1 + a:1 + a + chunk2] = CC[7, a:a + chunk2] * b[a:a + chunk2]
        for a in range(0, nx, chunk2):
            v = VC[1 + a:1 + a + chunk2] + CC[7, a:a + chunk2] * residual2(VC, b, a, chunk2)
            WC[1 + a:1 + a + chunk2] = v
        own = WC[pl.ds(1 + gx, 1)][0]
        for a in range(0, nx, chunk2):
            r = residual2(WC, b, a, chunk2)
            for i in range(chunk2):
                summed[a + i] = pooled(r[i])
        return own

    wait_group(G_BD, n_bd)
    own_c = down2(BC, PC)

    shape = (8, 128)
    half = lane // 64
    at_x = sub + 8 * half
    z = lax.rem(lane, 32)
    first_rhs = lax.rem(lane, 64) < 32

    def next_x(v):
        a = roll(v, -1, 1)
        return jnp.where(sub == 7, roll(a, 64, 2), a)

    def previous_x(v):
        a = roll(v, 1, 1)
        return jnp.where(sub == 0, roll(a, 64, 2), a)

    wait_group(G_BF, n_bf)
    own_f = down2(BF, PF)
    for i in range(nx):
        ZB[i:i + 1, :] = 0.5 * pair_lanes(jnp.where(even, PF[i], PC[i]), None)[0:1]
    GB[gy] = packed(ZB)
    n_gb = ship_row(G_GB, GB)
    U2[1, 4, 0:2, :] = jnp.where(even, own_f, roll(own_c, 64, 1))[0:2]
    U2[1, 5, 0:2, :] = jnp.where(even, roll(own_f, 64, 1), own_c)[0:2]
    n_u2 = ship(G_U2, U2, (0, 2), AROUND, 2, (4, 4), (4, 4), 4)
    wait_group(G_GK, n_gk)
    chunk3 = min(8, ny)
    for a in range(0, ny, chunk3):
        k = GK[a:a + chunk3]
        up_y = [GK[j] if j < ny else blank for j in range(a + 1, a + chunk3 + 1)]
        down_y = [GK[j] if j >= 0 else blank for j in range(a - 1, a + chunk3 - 1)]
        y_next = 0.5 * (k + jnp.stack(up_y))
        y_previous = 0.5 * (k + jnp.stack(down_y))
        x_next = 0.5 * (k + jnp.where(at_x < nx - 1, next_x(k), 0.0))
        x_previous = 0.5 * (k + jnp.where(at_x > 0, previous_x(k), 0.0))
        z_next = 0.5 * (k + jnp.where(z < 31, roll(k, -1, 2), 0.0))
        z_previous = 0.5 * (k + jnp.where(z > 0, roll(k, 1, 2), 0.0))
        C3[0, a:a + chunk3] = y_previous
        C3[1, a:a + chunk3] = y_next
        C3[2, a:a + chunk3] = jnp.where(at_x < nx - 1, x_next, 0.0)
        C3[3, a:a + chunk3] = jnp.where((at_x > 0) & (at_x < nx), x_previous, 0.0)
        C3[4, a:a + chunk3] = jnp.where(z < 31, z_next, 0.0)
        C3[5, a:a + chunk3] = jnp.where(z > 0, z_previous, 0.0)
        C3[6, a:a + chunk3] = y_next + y_previous + x_next + x_previous + z_next + z_previous
    R3[0] = blank
    R3[ny + 1] = blank
    for a in range(0, ny, chunk3):
        P3[a:a + chunk3] = jnp.zeros((chunk3,) + shape, F32)
        Q3[a:a + chunk3] = jnp.zeros((chunk3,) + shape, F32)
        X3[2 + a:2 + a + chunk3] = jnp.zeros((chunk3,) + shape, F32)
    wait_group(G_GB, n_gb)
    for a in range(0, ny, chunk3):
        R3[1 + a:1 + a + chunk3] = GB[a:a + chunk3]

    def over_grid(x):
        x = jnp.sum(x, axis=0, keepdims=True)
        first = jnp.sum(jnp.where(first_rhs[0:1], x, 0.0), axis=1, keepdims=True)
        second = jnp.sum(jnp.where(first_rhs[0:1], 0.0, x), axis=1, keepdims=True)
        return jnp.where(first_rhs[0:1], first, second)

    def iteration(_, carry):
        norm_before, alpha_before = carry
        norm, energy = blank, blank
        for a in range(0, ny, chunk3):
            mid = R3[1 + a:1 + a + chunk3]
            beside = C3[0, a:a + chunk3] * R3[a:a + chunk3] + C3[1, a:a + chunk3] * R3[2 + a:2 + a + chunk3]
            beside += C3[2, a:a + chunk3] * next_x(mid) + C3[3, a:a + chunk3] * previous_x(mid)
            beside += C3[4, a:a + chunk3] * roll(mid, -1, 2) + C3[5, a:a + chunk3] * roll(mid, 1, 2)
            image = C3[6, a:a + chunk3] * mid - beside
            W3[a:a + chunk3] = image
            norm += jnp.sum(mid * mid, axis=0)
            energy += jnp.sum(mid * image, axis=0)
        norm, energy = over_grid(norm), over_grid(energy)
        beta = norm / norm_before
        alpha = norm / (energy - beta * norm / alpha_before)
        for a in range(0, ny, chunk3):
            p = R3[1 + a:1 + a + chunk3] + beta * P3[a:a + chunk3]
            q = W3[a:a + chunk3] + beta * Q3[a:a + chunk3]
            P3[a:a + chunk3] = p
            Q3[a:a + chunk3] = q
            X3[2 + a:2 + a + chunk3] += alpha * p
            R3[1 + a:1 + a + chunk3] -= alpha * q
        return norm, alpha

    lax.fori_loop(0, CSWEEPS, iteration, (jnp.full((1, 128), jnp.inf, F32), jnp.ones((1, 128), F32)))

    near = X3[pl.ds(gy, 5)]
    S5[:, 2:10, :] = near
    S5[:, 10:18, :] = roll(near, 64, 2)
    for dx in range(-2, 3):
        for dy in range(-2, 3):
            T5[dx + 2, pl.ds(dy % ROWS, 1), :] = S5[dy + 2, pl.ds(gx + (dx + 2), 1), :]

    lane2 = lane // 2
    row_low, row_high = sub // 2, 4 + sub // 2

    wait_group(G_U2, n_u2)
    for i in range(5):
        low = take_rows(take_lanes(T5[i, 0:8], lane2), row_low)
        high = take_rows(take_lanes(T5[i, 8:16], lane2), row_high)
        for p in (2 * i, 2 * i + 1):
            v = U2[1, p] + jnp.concatenate([low, high], axis=0)
            M2[p:p + 1] = jnp.where(inside((1, ROWS, 128), p - 4, 2, 4), v[None], 0.0)
    sweep(at(M2, 4), 4, at(U2, 4, 0), C2, 3, to(VA2, 3), -3, 8, 4)
    sweep(at(VA2, 3), 3, at(U2, 4, 0), C2, 3, to(VB2, 2), -2, 6, 6)

    wait_group(G_V1, n_v1)
    for p1 in range(-3, 7):
        e = VB2[p1 // 2 + 2]
        good = inside((1, ROWS, 128), p1, 4, 3)
        for k in range(2):
            index = lane2 + 64 * k
            low = take_rows(take_lanes(e[0:8], index), row_low)
            high = take_rows(take_lanes(e[8:16], index), row_high)
            v = V1[k, p1 + 3] + jnp.concatenate([low, high], axis=0)
            M1[k, p1 + 3:p1 + 4] = jnp.where(good, v[None], 0.0)
    b1 = (at(V1, 3, 2), at(E1, 3, 0))
    for k in range(2):
        sweep(at(M1, 3, k), 3, b1[k], C1, 2, to(VA1, 2, k), -2, 8, 4)
    sweep(at(VA1, 2, 0), 2, b1[0], C1, 2, to(VB1, 1, 0), -1, 6, 6)

    def store_coarse(p, n, x):
        coarse_ref[pl.ds(p, n)] = x[:, 0:4]

    sweep(at(VA1, 2, 1), 2, b1[1], C1, 2, store_coarse, 0, 4, 4, 8)

    wait_group(G_V0, n_v0)
    for p1 in range(-1, 5):
        e = VB1[0, p1 + 1]
        pieces = []
        for k in range(2):
            index = lane2 + 64 * k
            first, second = take_lanes(e[0:8], index), take_lanes(e[8:16], index)
            low = take_rows(first, row_low)
            high = jnp.where(sub < 4, take_rows(first, row_high), take_rows(second, row_high))
            pieces.append(jnp.concatenate([low, high], axis=0))
        e = jnp.concatenate(pieces, axis=1)
        v = V0[2 * p1 + 2:2 * p1 + 4] + e[None]
        VA0[2 * p1 + 4:2 * p1 + 6] = jnp.where(inside(v.shape, 2 * p1, 8, 2), v, 0.0)
    sweep(at(VA0, 4), 4, at(S0, 4), C0, 4, to(VB0, 3), -1, 10, 2)
    sweep(at(VB0, 3), 3, at(S0, 4), C0, 4, to(fine_ref, 0), 0, 8, 2, 8)

    for group, rows in ((G_K0, n_k0), (G_S0, n_s0), (G_E1, n_e1), (G_K2, n_k2), (G_KC, n_kc), (G_KD, n_kd), (G_BD, n_bd), (G_GK, n_gk), (G_B1, n_b1),
                        (G_BF, n_bf), (G_BC, n_bc), (G_GB, n_gb), (G_V0, n_v0), (G_V1, n_v1), (G_U2, n_u2)):
        wait_rows(rows, send_sem.at[group])


def put_out(fine, coarse, fine_out, coarse_out, sem):
    copies = [
        pltpu.make_async_copy(fine, fine_out, sem.at[0]),
        pltpu.make_async_copy(coarse, coarse_out, sem.at[1]),
    ]
    for copy in copies:
        copy.start()
    for copy in copies:
        copy.wait()


def solution(mesh):
    nx, ny = mesh.shape["gx"], mesh.shape["gy"]

    def vmem(*shape):
        return pltpu.VMEM(shape, F32)

    def on_device(source, kappa):
        scratch = [
            vmem(18, 16, 256), vmem(16, 16, 256), vmem(12, 16, 256), vmem(16, 16, 256), vmem(14, 16, 256),
            vmem(7, 17, 16, 256),
            vmem(2, 10, 16, 128), vmem(10, 16, 128), vmem(3, 10, 16, 128), vmem(2, 8, 16, 128), vmem(2, 6, 16, 128),
            vmem(7, 9, 16, 128), vmem(2, 10, 16, 128),
            vmem(10, 16, 128), vmem(2, 10, 16, 128), vmem(8, 16, 128), vmem(6, 16, 128),
            vmem(7, 9, 16, 128), vmem(10, 16, 128),
            vmem(nx, 8, 128), vmem(nx, 8, 128), vmem(nx, 8, 128),
            vmem(nx + 2, 8, 128), vmem(nx + 2, 8, 128), vmem(nx + 2, 8, 128),
            vmem(nx, 8, 128), vmem(nx, 8, 128), vmem(8, nx, 8, 128),
            vmem(16, 128), vmem(16, 128), vmem(ny, 8, 128), vmem(ny, 8, 128),
            vmem(7, ny, 8, 128), vmem(ny + 2, 8, 128), vmem(ny, 8, 128), vmem(ny, 8, 128), vmem(ny, 8, 128),
            vmem(ny + 4, 8, 128), vmem(5, 24, 128), vmem(5, 16, 128),
            vmem(512, 128),
            pltpu.SemaphoreType.DMA((2,)), pltpu.SemaphoreType.DMA((GROUPS,)), pltpu.SemaphoreType.DMA((GROUPS,)), pltpu.SemaphoreType.REGULAR((10,)),
        ]
        fine, coarse = pl.pallas_call(
            lambda *refs: kernel(nx, ny, *refs),
            out_shape=(jax.ShapeDtypeStruct((8, 8, 256), F32), jax.ShapeDtypeStruct((4, 4, 128), F32)),
            in_specs=[pl.BlockSpec(memory_space=pltpu.HBM)] * 2,
            out_specs=[pl.BlockSpec(memory_space=pltpu.VMEM)] * 2,
            scratch_shapes=scratch,
            compiler_params=pltpu.CompilerParams(
                collective_id=0, has_side_effects=True, vmem_limit_bytes=32 * 1024 * 1024
            ),
            name="vcycles",
        )(*(pltpu.with_memory_space_constraint(x, pltpu.HBM) for x in (source, kappa)))
        return pl.pallas_call(
            put_out,
            out_shape=(jax.ShapeDtypeStruct((8, 8, 256), F32), jax.ShapeDtypeStruct((4, 4, 128), F32)),
            in_specs=[pl.BlockSpec(memory_space=pltpu.VMEM)] * 2,
            out_specs=[pl.BlockSpec(memory_space=pltpu.HBM)] * 2,
            scratch_shapes=[pltpu.SemaphoreType.DMA((2,))],
            compiler_params=pltpu.CompilerParams(vmem_limit_bytes=4 * 1024 * 1024),
            name="put_out",
        )(fine, coarse)

    spec = P("gx", "gy", None)
    return jax.shard_map(on_device, mesh=mesh, in_specs=(spec, spec), out_specs=(spec, spec), check_vma=False)
```
